128 devices in a mesh: ctx: 64 (over z, x, y_lo, core), ch: 2 (over y_hi).
Axes of the slice: x: 4, y: 4 (y_hi: 2, y_lo: 2; y = y_hi * 2 + y_lo), z: 4, core: 2. Of those that a mesh axis runs over, the one named last changes fastest.
Arguments:
- rollout_rows: bfloat16 [384, 128, 3, 2048], P('ctx', None, None, 'ch'), may hold values from -6 to 6
- pack_targets: int32 [384, 2], replicated, may hold values from -1 to 63, as said below
- doc_lengths: int32 [128], replicated, may hold values from 1 to 2049, 32768 in all
- filter_taps: float32 [4, 2049], replicated, may hold values from -3 to 3
- skip_gain: float32 [2048], P('ch'), may hold values from 0.1 to 1.9
- out_grad: bfloat16 [32768, 2048], P('ctx', 'ch'), may hold values from -6 to 6
Outputs:
- out_y: bfloat16 [32768, 2048], P('ctx', 'ch')
- grad_streams: bfloat16 [32768, 3, 2048], P('ctx', None, 'ch')
- grad_taps: float32 [4, 2049], replicated
- grad_skip: float32 [2048], P('ch')
The draws below stay inside these ranges and needn't reach their ends.
Inputs may be any that keep to these rules, and one draw needn't show every extreme that they name: `pack_targets`: owner of slot g is g // 6. Every pair (shard, offset) with offset below 4 is named by exactly one slot; a named shard is the owner itself or one of its two neighbours on the closed cycle of context shards (shard 0 and the last are neighbours). One owner gives at most 1 row to one neighbouring shard, and in every draw some owner gives exactly 1 row to the shard below it and some owner, possibly another, gives exactly 1 row to the shard above it. Unused slots hold (-1, -1). `doc_lengths`: the documents fill all 32768 positions; the longest has exactly 2049 tokens.
All inputs are finite; a program needn't handle non-finite values.
Results may differ from the reference program's by a relative error of at most 0.01.
Values may be sent and summed in bfloat16 or wider, within the bound.
No kernel may reach another device: no remote copies, remote signals or barrier semaphores. Data moves between devices by JAX's collectives and lax.ppermute only.
A program may use at most 128 MiB of HBM per device.

```python
import math
import jax
import jax.numpy as jnp
import numpy as np
from jax import lax

CW = 2048
NF = 4
FL = 2048
ROW = 128
TOK_DEV = 512
RPD = 4
BL = 256
CAPS = 1
OWN_CAP = 6
BLOCKS = 128
SEQ = 32768
NDOC = 128
DOC_MOST = 2049
CB = 256
N_CTX = 64
N_CH = 2


def draw_pack_targets(key, part):
    owners = BLOCKS // 2
    key_list = jax.random.split(jax.random.fold_in(key, 11), 6)
    from_below = jax.random.randint(key_list[0], (owners,), 0, CAPS + 1)
    from_above = jax.random.randint(key_list[1], (owners,), 0, CAPS + 1)
    pick_below = jax.random.randint(key_list[2], (), 0, owners)
    pick_above = jax.random.randint(key_list[3], (), 0, owners)
    from_below = from_below.at[pick_below].set(CAPS)
    from_above = from_above.at[pick_above].set(CAPS)
    orders = jax.vmap(lambda sub_key: jax.random.permutation(sub_key, RPD))(jax.random.split(key_list[4], owners)).astype(jnp.int32)
    owner_ids = jnp.arange(owners)
    below_ids = (owner_ids + owners - 1) % owners
    above_ids = (owner_ids + 1) % owners
    lane_ids = jnp.arange(CAPS)
    own_lanes = jnp.arange(RPD)
    live_down = lane_ids[None, :] < from_above[below_ids][:, None]
    offset_down = jnp.take_along_axis(orders[below_ids], jnp.clip(from_below[below_ids][:, None] + lane_ids[None, :], 0, RPD - 1), axis=1)
    live_up = lane_ids[None, :] < from_below[above_ids][:, None]
    offset_up = jnp.take_along_axis(orders[above_ids], jnp.clip(jnp.broadcast_to(lane_ids[None, :], (owners, CAPS)), 0, RPD - 1), axis=1)
    own_count = RPD - from_below - from_above
    live_own = own_lanes[None, :] < own_count[:, None]
    offset_own = jnp.take_along_axis(orders, jnp.clip(from_below[:, None] + from_above[:, None] + own_lanes[None, :], 0, RPD - 1), axis=1)
    shard_table = jnp.concatenate([jnp.where(live_down, below_ids[:, None], -1), jnp.where(live_up, above_ids[:, None], -1), jnp.where(live_own, owner_ids[:, None], -1)], axis=1)
    offset_table = jnp.concatenate([jnp.where(live_down, offset_down, -1), jnp.where(live_up, offset_up, -1), jnp.where(live_own, offset_own, -1)], axis=1)
    slot_order = jax.vmap(lambda sub_key: jax.random.permutation(sub_key, OWN_CAP))(jax.random.split(key_list[5], owners))
    shard_table = jnp.take_along_axis(shard_table, slot_order, axis=1)
    offset_table = jnp.take_along_axis(offset_table, slot_order, axis=1)
    return jnp.stack([shard_table, offset_table], axis=-1).reshape(owners * OWN_CAP, 2).astype(jnp.int32)


def draw_filter_taps(key, part):
    key_list = jax.random.split(jax.random.fold_in(key, 23), 2)
    lag_ids = jnp.arange(FL + 1).astype(jnp.float32)[None, :]
    upper = math.log(max(4.0 * FL, 120.0))
    decay_len = jnp.exp(jax.random.uniform(key_list[0], (NF, 1), jnp.float32, math.log(30.0), upper))
    noise = jax.random.truncated_normal(key_list[1], -4.0, 4.0, (NF, FL + 1), jnp.float32)
    ratio_sq = jnp.exp(-2.0 / decay_len)
    amplitude = jnp.sqrt((1.0 - ratio_sq) / (1.0 - ratio_sq ** (FL + 1)))
    envelope = jnp.exp(-lag_ids / decay_len) * amplitude
    taps_out = noise * envelope
    return taps_out.astype(jnp.float32)


def block_scale(rng, dims, shards, low, high):
    def one(axis_at, shards_of):
        draws = jax.random.uniform(jax.random.fold_in(jax.random.fold_in(rng, 6), axis_at), (shards_of,), jnp.float32, low / len(shards), high / len(shards))
        return jnp.repeat(jnp.exp(draws), dims[axis_at] // shards_of).reshape((-1,) + (1,) * (len(dims) - axis_at - 1))

    loudness = one(*shards[0])
    for cut in shards[1:]:
        loudness = loudness * one(*cut)
    return loudness


def profile(number_of, total, bound, lean):
    weights = [(1 << 20) // math.isqrt(rank ** lean) + 1 for rank in range(2, number_of + 1)]
    surplus, counts = total - bound - (number_of - 1), [1] * (number_of - 1)
    while surplus > 0:
        free = [i for i in range(number_of - 1) if counts[i] < bound]
        whole, budget = sum([weights[i] for i in free]), surplus
        for i in free:
            more = min(bound - counts[i], max(1, budget * weights[i] // whole), surplus)
            counts[i] = counts[i] + more
            surplus = surplus - more
    return np.array([bound] + counts)


def uneven(stream_key, number_of, total, bound, skew):
    if number_of == 2:
        one = jax.random.randint(stream_key, (), max(1, total - bound), min(bound, total - 1) + 1)
        return jnp.stack([one, total - one])
    sizes = jnp.asarray(profile(number_of, total, bound, skew), jnp.int32)
    couples = (number_of - 1) // 2
    donor, sink = sizes[1:1 + 2 * couples:2], sizes[2:2 + 2 * couples:2]
    slack = jnp.minimum(donor - 1, bound - sink)
    shifted = jax.random.randint(jax.random.fold_in(stream_key, 1), (couples,), 0, 1 << 20) % (slack + 1)
    sizes = sizes.at[1:1 + 2 * couples:2].set(donor - shifted).at[2:2 + 2 * couples:2].set(sink + shifted)
    return sizes[jax.random.permutation(jax.random.fold_in(stream_key, 2), number_of)]


def scatter_about(key, extent, deviation, limit, cuts=(), held_as=jnp.bfloat16):
    drawn = jax.random.normal(key, extent, jnp.float32) * deviation
    if len(cuts) > 0:
        drawn = block_scale(key, extent, cuts, -0.22, 0.18) * drawn
    return jnp.clip(drawn, min=-limit, max=limit).astype(held_as)


def setup_inputs(seed: int = 0) -> dict:
    keys = jax.random.split(jax.random.key(seed), 7)
    return {
        "rollout_rows": scatter_about(keys[0], (N_CTX * OWN_CAP, ROW, 3, CW), 1.0, 6.0, ((0, 64), (3, 2))),
        "pack_targets": draw_pack_targets(jax.random.fold_in(keys[6], 71), 0),
        "doc_lengths": uneven(keys[2], NDOC, SEQ, DOC_MOST, 2).astype(jnp.int32),
        "filter_taps": draw_filter_taps(jax.random.fold_in(keys[6], 71), 0),
        "skip_gain": jnp.clip(1.0 + 0.18 * jax.random.normal(keys[4], (CW,), jnp.float32), 0.1, 1.9),
        "out_grad": scatter_about(keys[5], (SEQ, CW), 1.0, 6.0, ((0, 64), (1, 2))),
    }


def to_sequence(stored):
    blocks = stored.reshape((N_CTX, 2, TOK_DEV // 2) + stored.shape[1:])
    joined = jnp.concatenate([blocks[:, 0], blocks[::-1, 1]], axis=0)
    return joined.reshape(stored.shape)

def to_storage(ordered):
    blocks = ordered.reshape((2 * N_CTX, TOK_DEV // 2) + ordered.shape[1:])
    joined = jnp.stack([blocks[:N_CTX], blocks[N_CTX:][::-1]], axis=1)
    return joined.reshape(ordered.shape)

def doc_begin_of(positions, starts):
    found = jnp.searchsorted(starts, positions, side='right').astype(jnp.int32) - 1
    return starts[jnp.clip(found, 0, NDOC - 1)]

def reference(rollout_rows, pack_targets, doc_lengths, filter_taps, skip_gain, out_grad):
    live_slot = pack_targets[:, 0] >= 0
    destination = jnp.where(live_slot, pack_targets[:, 0] * RPD + pack_targets[:, 1], N_CTX * RPD).astype(jnp.int32)
    packed = jnp.zeros((N_CTX * RPD, ROW, 3, CW), jnp.bfloat16).at[destination].set(rollout_rows, mode='drop')
    streams = to_sequence(packed.reshape(SEQ, 3, CW))
    query_f = streams[:, 0].astype(jnp.float32)
    keys_f = streams[:, 1].astype(jnp.float32)
    values_f = streams[:, 2].astype(jnp.float32)
    product = (keys_f * values_f).astype(jnp.bfloat16)
    product_f = product.astype(jnp.float32)
    grad_f = to_sequence(out_grad).astype(jnp.float32)
    grad_mid = (grad_f * query_f).astype(jnp.bfloat16).astype(jnp.float32)
    starts = (jnp.cumsum(doc_lengths) - doc_lengths).astype(jnp.int32)
    taps = filter_taps.astype(jnp.bfloat16).astype(jnp.float32)
    row_ids = jnp.arange(BL, dtype=jnp.int32)[:, None]
    col_ids = jnp.arange(FL + BL, dtype=jnp.int32)[None, :]
    fwd_lag = row_ids - col_ids + FL
    fwd_valid = (fwd_lag >= 0) & (fwd_lag <= FL)
    fwd_band = jnp.where(fwd_valid[None], taps[:, jnp.clip(fwd_lag, 0, FL)], 0.0)
    bwd_lag = col_ids - row_ids
    bwd_valid = (bwd_lag >= 0) & (bwd_lag <= FL)
    bwd_band = jnp.where(bwd_valid[None], taps[:, jnp.clip(bwd_lag, 0, FL)], 0.0)
    padded_x = jnp.concatenate([jnp.zeros((FL, CW), jnp.float32), product_f], axis=0)
    padded_g = jnp.concatenate([grad_mid, jnp.zeros((FL, CW), jnp.float32)], axis=0)

    def one_tile(tile):
        base = (tile * BL).astype(jnp.int32)
        near = base + jnp.arange(BL, dtype=jnp.int32)
        far_back = base - FL + jnp.arange(FL + BL, dtype=jnp.int32)
        far_ahead = base + jnp.arange(FL + BL, dtype=jnp.int32)
        fwd_keep = far_back[None, :] >= doc_begin_of(near, starts)[:, None]
        bwd_keep = near[:, None] >= doc_begin_of(far_ahead, starts)[None, :]
        sources = lax.dynamic_slice_in_dim(padded_x, base, FL + BL, 0).reshape(FL + BL, N_CH, NF, CB)
        ahead_g = lax.dynamic_slice_in_dim(padded_g, base, FL + BL, 0).reshape(FL + BL, N_CH, NF, CB)
        own_g = lax.dynamic_slice_in_dim(grad_mid, base, BL, 0).reshape(BL, N_CH, NF, CB)
        fwd_mat = jnp.where(fwd_keep[None], fwd_band, 0.0)
        bwd_mat = jnp.where(bwd_keep[None], bwd_band, 0.0)
        conv_tile = jnp.einsum('fij,jgfc->igfc', fwd_mat, sources)
        back_tile = jnp.einsum('fij,jgfc->igfc', bwd_mat, ahead_g)
        pairs = jnp.einsum('igfc,jgfc->fij', own_g, sources)
        pairs = jnp.where((fwd_keep & fwd_valid)[None], pairs, 0.0)
        tap_tile = jnp.zeros((NF, FL + 1), jnp.float32).at[:, jnp.clip(fwd_lag, 0, FL)].add(pairs)
        return (conv_tile.reshape(BL, CW), back_tile.reshape(BL, CW), tap_tile)
    conv_all, back_all, tap_all = lax.map(one_tile, jnp.arange(SEQ // BL, dtype=jnp.int32))
    mixed = conv_all.reshape(SEQ, CW) + skip_gain[None, :] * product_f
    out_y = (query_f * mixed).astype(jnp.bfloat16)
    grad_query = (grad_f * mixed).astype(jnp.bfloat16)
    grad_x = back_all.reshape(SEQ, CW) + skip_gain[None, :] * grad_mid
    grad_key = (grad_x * values_f).astype(jnp.bfloat16)
    grad_value = (grad_x * keys_f).astype(jnp.bfloat16)
    grad_streams = jnp.stack([grad_query, grad_key, grad_value], axis=1)
    grad_taps = lax.optimization_barrier(jnp.sum(tap_all, axis=0)) / math.sqrt(SEQ * CW / NF)
    grad_skip = lax.optimization_barrier(jnp.sum(grad_mid * product_f, axis=0)) / math.sqrt(SEQ)
    return (to_storage(out_y), to_storage(grad_streams), grad_taps, grad_skip)
```

```python
import functools
import math

import jax
import jax.numpy as jnp
from jax import lax
from jax.experimental import pallas as pl
from jax.experimental.pallas import tpu as pltpu
from jax.sharding import PartitionSpec as P

BF16 = jnp.bfloat16
F32 = jnp.float32
SMEM = pltpu.SMEM
VMEM = pltpu.VMEM

BLK = 256
HOPS = 8
SLOTS = 6
ROWS = 4
LANES = 128
VLIM = 56 * 1024 * 1024


def smem():
    return pl.BlockSpec(memory_space=SMEM)


def vmem():
    return pl.BlockSpec(memory_space=VMEM)


def choose_kernel(cycle, me_ref, target_ref, own_ref, up_ref, down_ref, code_ref, slot_ref, sems):
    me = me_ref[0]
    below = lax.rem(me + cycle - 1, cycle)
    above = lax.rem(me + 1, cycle)
    up_slot = jnp.int32(0)
    down_slot = jnp.int32(0)
    for o in range(ROWS):
        code_ref[o] = 0
        slot_ref[o] = 0
    for k in range(SLOTS):
        shard = target_ref[0, me * SLOTS + k]
        offset = target_ref[1, me * SLOTS + k]
        up_slot = jnp.where(shard == above, k, up_slot)
        down_slot = jnp.where(shard == below, k, down_slot)

        @pl.when(shard == me)
        def _():
            slot_ref[offset] = k

        for owner, code in ((below, 1), (above, 2)):
            their_shard = target_ref[0, owner * SLOTS + k]
            their_offset = target_ref[1, owner * SLOTS + k]

            @pl.when(their_shard == me)
            def _():
                code_ref[their_offset] = code

    up = pltpu.make_async_copy(own_ref.at[up_slot], up_ref, sems.at[0])
    down = pltpu.make_async_copy(own_ref.at[down_slot], down_ref, sems.at[1])
    up.start()
    down.start()
    up.wait()
    down.wait()


def tables_kernel(docs, length_ref, taps_ref, table_ref, fwd_ref, bwd_ref):
    def one_doc(d, start):
        end = start + length_ref[d]
        table_ref[3, d] = start
        table_ref[4, d] = end

        def heads(b, carry):
            table_ref[0, b] = b - lax.shift_right_logical(start, 8)
            table_ref[1, b] = jnp.minimum(end - BLK * b, BLK)
            return carry

        def tails(b, carry):
            table_ref[2, b] = jnp.maximum(start - BLK * b, 0)
            return carry

        lax.fori_loop(
            lax.shift_right_logical(start + BLK - 1, 8),
            lax.shift_right_logical(end + BLK - 1, 8),
            heads,
            0,
        )
        lax.fori_loop(
            lax.shift_right_logical(start, 8), lax.shift_right_logical(end, 8), tails, 0
        )
        return end

    lax.fori_loop(0, docs, one_doc, jnp.int32(0))
    width = BLK * (HOPS + 2)
    part = 32
    for r in range(BLK // part):
        rows = jnp.broadcast_to(taps_ref[...], (part, width))
        rows = pltpu.roll(rows, part * r, 1, stride=1, stride_axis=0)
        for delta in range(HOPS + 1):
            at = BLK * (HOPS - delta) + part * r
            fwd_ref[at : at + part, :] = rows[:, BLK * (delta + 1) : BLK * (delta + 2)].astype(BF16)
    for delta in range(HOPS + 1):
        at = BLK * (HOPS - delta)
        bwd_ref[BLK * delta : BLK * (delta + 1), :] = fwd_ref[at : at + BLK, :].T


def pick(code, own_ref, low_ref, high_ref, stream):
    own = own_ref[0, stream]
    low = low_ref[stream]
    high = high_ref[stream]
    return jnp.where(code == 0, own, jnp.where(code == 1, low, high))


def round_mul(a, b):
    return (a.astype(F32) * b.astype(F32)).astype(BF16)


def make_kernel(code_ref, slot_ref, own_ref, low_ref, high_ref, grad_ref, sent_ref):
    code = code_ref[pl.program_id(0)]

    def emit(read):
        product = round_mul(read(1), read(2))
        grad_mid = round_mul(grad_ref[...], read(0))
        peers, _, chans, toks = sent_ref.shape
        sent_ref[:, 0] = product.T.reshape(peers, chans, toks)
        sent_ref[:, 1] = grad_mid.T.reshape(peers, chans, toks)

    pl.when(code == 0)(lambda: emit(lambda s: own_ref[0, s]))
    pl.when(code == 1)(lambda: emit(lambda s: low_ref[s]))
    pl.when(code == 2)(lambda: emit(lambda s: high_ref[s]))


def place_of(b, peers):
    src = jnp.where(b < peers, b, 2 * peers - 1 - b)
    lane = pl.multiple_of(jnp.where(b < peers, 0, BLK), BLK)
    return src, lane


def long_kernel(
    table_ref, got_ref, fwd_ref, bwd_ref, out_ref,
    x_all, z_all, x_tail, z_head, reach, head_end, tail_start,
    xd, zd, ze, flip_all, flip_head, flip_doc, conv, back, pairs, extra,
):
    peers = got_ref.shape[0]
    ch = got_ref.shape[2]
    blocks = 2 * peers
    docs = blocks
    rows = blocks * ch
    pad = HOPS * ch
    lane = lax.broadcasted_iota(jnp.int32, (ch, BLK), 1)
    zero = jnp.zeros((), BF16)

    x_tail[0:pad, :] = jnp.zeros((pad, BLK), BF16)
    z_head[rows : rows + pad, :] = jnp.zeros((pad, BLK), BF16)
    reach[rows : rows + pad, :] = jnp.full((pad, BLK), -1, BF16)

    def spread(b, total):
        src, at_lane = place_of(b, peers)
        at = pl.multiple_of(b * ch, ch)
        x = got_ref[src, 0, :, pl.ds(at_lane, BLK)]
        z = got_ref[src, 1, :, pl.ds(at_lane, BLK)]
        x_all[pl.ds(at, ch), :] = x
        z_all[pl.ds(at, ch), :] = z
        first, end, tail = table_ref[0, b], table_ref[1, b], table_ref[2, b]
        x_f, z_f = x.astype(F32), z.astype(F32)
        x_tail[pl.ds(at + pad, ch), :] = jnp.where(lane >= tail, x_f, 0).astype(BF16)
        z_head[pl.ds(at, ch), :] = jnp.where(lane < end, z_f, 0).astype(BF16)
        reach[pl.ds(at, ch), :] = jnp.full((ch, BLK), first.astype(F32)).astype(BF16)
        head_end[pl.ds(at, ch), :] = jnp.full((ch, BLK), end, jnp.int32)
        tail_start[pl.ds(at, ch), :] = jnp.full((ch, BLK), tail, jnp.int32)
        return total + x_f * z_f

    skip = lax.fori_loop(0, blocks, spread, jnp.zeros((ch, BLK), F32))

    def doc_parts(d):
        start, end = table_ref[3, d], table_ref[4, d]
        end_block = lax.shift_right_logical(end - 1, 8)
        end_at = jnp.bitwise_and(end, BLK - 1)
        end_from = jnp.maximum(start - BLK * end_block, 0)
        start_block = lax.shift_right_logical(start, 8)
        start_at = jnp.bitwise_and(start, BLK - 1)
        start_at = jnp.where(start_at == 0, BLK, start_at)
        start_to = end - BLK * start_block
        return end_block, end_from, end_at, start_block, start_at, start_to

    def spread_docs(d, carry):
        end_block, end_from, end_at, start_block, start_at, start_to = doc_parts(d)
        at = pl.multiple_of(d * ch, ch)
        at_end = pl.multiple_of(end_block * ch, ch)
        at_start = pl.multiple_of(start_block * ch, ch)
        ends = (lane >= end_from) & (lane < end_at)
        begins = (lane >= start_at) & (lane < start_to)
        x = x_all[pl.ds(at_end, ch), :].astype(F32)
        z = z_all[pl.ds(at_end, ch), :].astype(F32)
        z2 = z_all[pl.ds(at_start, ch), :].astype(F32)
        xd[pl.ds(at, ch), :] = jnp.where(ends, x, 0).astype(BF16)
        zd[pl.ds(at, ch), :] = jnp.where(ends, z, 0).astype(BF16)
        ze[pl.ds(at, ch), :] = jnp.where(begins, z2, 0).astype(BF16)
        return carry

    lax.fori_loop(0, docs, spread_docs, 0)

    r_id = lax.broadcasted_iota(jnp.int32, (BLK, BLK), 0)
    c_id = lax.broadcasted_iota(jnp.int32, (BLK, BLK), 1)
    anti = jnp.where(r_id + c_id == BLK - 1, 1.0, 0.0).astype(BF16)
    step = 256
    steps = rows // step

    def flips(c, carry):
        at = pl.multiple_of(c * step, step)
        for src, dst in ((z_all, flip_all), (z_head, flip_head), (zd, flip_doc)):
            dst[:, pl.ds(at, step)] = lax.dot_general(
                anti, src[pl.ds(at, step), :], (((1,), (1,)), ((), ())),
                preferred_element_type=F32,
            ).astype(BF16)
        return carry

    lax.fori_loop(0, steps, flips, 0)
    pairs[...] = jnp.zeros_like(pairs)
    wide = lax.broadcasted_iota(jnp.int32, (step, BLK), 1)
    far = HOPS * BLK

    def dot(a, b):
        return jnp.dot(a, b, preferred_element_type=F32)

    def chunk(c, carry):
        at = pl.multiple_of(c * step, step)
        here = reach[pl.ds(at, step), :]
        xs = []
        for delta in range(HOPS, -1, -1):
            x = x_tail[pl.ds(at + ch * (HOPS - delta), step), :]
            xs.append(jnp.where(here >= delta, x, zero) if delta else x)
        x_far = jnp.concatenate(xs[:-1], axis=1)
        far_part = dot(x_far, fwd_ref[0:far, :])
        far_part = jnp.where(wide < head_end[pl.ds(at, step), :], far_part, 0.0)
        conv[pl.ds(at, step), :] = far_part + dot(xs[-1], fwd_ref[far:, :])
        pairs[:, 0:far] += dot(flip_head[:, pl.ds(at, step)], x_far)
        pairs[:, far:] += dot(flip_all[:, pl.ds(at, step)], xs[-1]) + dot(
            flip_doc[:, pl.ds(at, step)], xd[pl.ds(at, step), :]
        )
        zs = []
        for delta in range(HOPS + 1):
            z = z_head[pl.ds(at + ch * delta, step), :]
            there = reach[pl.ds(at + ch * delta, step), :]
            zs.append(jnp.where(there >= delta, z, zero) if delta else z)
        z_far = jnp.concatenate(zs[1:], axis=1)
        far_part = dot(z_far, bwd_ref[BLK:, :])
        far_part = jnp.where(wide >= tail_start[pl.ds(at, step), :], far_part, 0.0)
        back[pl.ds(at, step), :] = far_part + dot(zs[0], bwd_ref[0:BLK, :])
        return carry

    lax.fori_loop(0, steps, chunk, 0)

    def doc_chunk(c, carry):
        at = pl.multiple_of(c * step, step)
        y_end = dot(xd[pl.ds(at, step), :], fwd_ref[far:, :])
        y_start = dot(ze[pl.ds(at, step), :], bwd_ref[0:BLK, :])
        for i in range(step // ch):
            d = c * (step // ch) + i
            end_block, end_from, end_at, start_block, start_at, start_to = doc_parts(d)
            at_end = pl.multiple_of(end_block * ch, ch)
            at_start = pl.multiple_of(start_block * ch, ch)
            conv[pl.ds(at_end, ch), :] += jnp.where(
                lane < end_at, y_end[i * ch : (i + 1) * ch], 0.0
            )
            back[pl.ds(at_start, ch), :] += jnp.where(
                lane >= start_at, y_start[i * ch : (i + 1) * ch], 0.0
            )
        return carry

    lax.fori_loop(0, steps, doc_chunk, 0)

    def gather_out(b, carry):
        src, at_lane = place_of(b, peers)
        at = pl.multiple_of(b * ch, ch)
        out_ref[src, 0, :, pl.ds(at_lane, BLK)] = conv[pl.ds(at, ch), :].astype(BF16)
        out_ref[src, 1, :, pl.ds(at_lane, BLK)] = back[pl.ds(at, ch), :].astype(BF16)
        return carry

    lax.fori_loop(0, blocks, gather_out, 0)

    total = jnp.zeros((8, far + 2 * BLK), F32)
    for r in range(BLK // 8):
        band = jnp.concatenate([pairs[8 * r : 8 * (r + 1), :], jnp.zeros((8, BLK), F32)], axis=1)
        total = total + pltpu.roll(band, 8 * r, 1, stride=1, stride_axis=0)
    lags = jnp.sum(total, axis=0, keepdims=True)
    extra[...] = jnp.zeros_like(extra)
    count = (far + BLK) // LANES
    for r in range(count):
        extra[r : r + 1, :] = lags[:, LANES * r : LANES * (r + 1)]
    by_channel = jnp.sum(skip, axis=1, keepdims=True)
    e_row = lax.broadcasted_iota(jnp.int32, (ch, LANES), 0)
    e_col = lax.broadcasted_iota(jnp.int32, (ch, LANES), 1)
    skip_row = jnp.sum(jnp.where(e_row == e_col, by_channel, 0.0), axis=0, keepdims=True)
    high = skip_row.astype(BF16).astype(F32)
    extra[count : count + 1, :] = high
    extra[count + 1 : count + 2, :] = skip_row - high
    packed = extra[...].astype(BF16)
    for side in range(2):
        out_ref[:, side, :, 2 * BLK : 2 * BLK + LANES] = jnp.broadcast_to(
            packed[side * ch : (side + 1) * ch][None], (peers, ch, LANES)
        )


def finish_kernel(
    code_ref, slot_ref, own_ref, low_ref, high_ref, grad_ref, gain_ref, got_ref, y_ref, grads_ref
):
    code = code_ref[pl.program_id(0)]

    def emit(read):
        peers, _, chans, toks = got_ref.shape
        width = peers * chans
        conv = got_ref[:, 0].reshape(width, toks).T.astype(F32)
        back = got_ref[:, 1].reshape(width, toks).T.astype(F32)
        query, key_in, value = (read(s).astype(F32) for s in range(3))
        grad = grad_ref[...].astype(F32)
        gain = gain_ref[...]
        product = (key_in * value).astype(BF16).astype(F32)
        grad_mid = (grad * query).astype(BF16).astype(F32)
        mixed = conv + gain * product
        grad_x = back + gain * grad_mid
        y_ref[...] = (query * mixed).astype(BF16)
        grads_ref[0] = (grad * mixed).astype(BF16)
        grads_ref[1] = (grad_x * value).astype(BF16)
        grads_ref[2] = (grad_x * key_in).astype(BF16)

    pl.when(code == 0)(lambda: emit(lambda s: own_ref[0, s]))
    pl.when(code == 1)(lambda: emit(lambda s: low_ref[s]))
    pl.when(code == 2)(lambda: emit(lambda s: high_ref[s]))


def shifted(array, axis, by):
    length = lax.axis_size(axis)
    return lax.ppermute(array, axis, [(i, (i + by) % length) for i in range(length)])


def on_device(rollout_rows, pack_targets, doc_lengths, filter_taps, skip_gain, out_grad):
    peers = lax.axis_size("ctx")
    index = lax.axis_index("ctx").astype(jnp.int32)
    slots, row_len, streams, channels = rollout_rows.shape
    tokens = out_grad.shape[0]
    filters, tap_count = filter_taps.shape
    docs = doc_lengths.shape[0]
    ch = channels // peers
    blocks = 2 * peers
    own = rollout_rows.transpose(0, 2, 1, 3)
    row_shape = jax.ShapeDtypeStruct((streams, row_len, channels), BF16)

    any_spec = pl.BlockSpec(memory_space=pl.ANY)
    up, down, code, slot = pl.pallas_call(
        functools.partial(choose_kernel, peers),
        out_shape=(
            row_shape,
            row_shape,
            jax.ShapeDtypeStruct((ROWS,), jnp.int32),
            jax.ShapeDtypeStruct((ROWS,), jnp.int32),
        ),
        in_specs=[smem(), smem(), any_spec],
        out_specs=(any_spec, any_spec, smem(), smem()),
        scratch_shapes=[pltpu.SemaphoreType.DMA((2,))],
        name="choose",
    )(index[None], pack_targets.T, own)
    low = shifted(up, "ctx", 1)
    high = shifted(down, "ctx", -1)

    mine = lax.dynamic_index_in_dim(filter_taps, index // (peers // filters), 0, keepdims=True)
    mine = mine.astype(BF16).astype(F32)
    mine = jnp.pad(mine, [(0, 0), (BLK, BLK * (HOPS + 1) - tap_count)])
    band = jax.ShapeDtypeStruct((BLK * (HOPS + 1), BLK), BF16)
    table, fwd_band, bwd_band = pl.pallas_call(
        functools.partial(tables_kernel, docs),
        out_shape=(jax.ShapeDtypeStruct((8, docs), jnp.int32), band, band),
        in_specs=[smem(), vmem()],
        out_specs=(smem(), vmem(), vmem()),
        compiler_params=pltpu.CompilerParams(vmem_limit_bytes=VLIM),
        cost_estimate=pl.CostEstimate(flops=0, bytes_accessed=20_000_000, transcendentals=0),
        name="tables",
    )(doc_lengths, mine)

    def row_specs():
        return [
            pl.BlockSpec(
                (1, streams, row_len, channels), lambda o, code, slot: (slot[o], 0, 0, 0)
            ),
            pl.BlockSpec((streams, row_len, channels), lambda o, code, slot: (0, 0, 0)),
            pl.BlockSpec((streams, row_len, channels), lambda o, code, slot: (0, 0, 0)),
            pl.BlockSpec((row_len, channels), lambda o, code, slot: (o, 0)),
        ]

    sent = pl.pallas_call(
        make_kernel,
        out_shape=jax.ShapeDtypeStruct((peers, 2, ch, tokens), BF16),
        grid_spec=pltpu.PrefetchScalarGridSpec(
            num_scalar_prefetch=2,
            grid=(ROWS,),
            in_specs=row_specs(),
            out_specs=pl.BlockSpec((peers, 2, ch, row_len), lambda o, code, slot: (0, 0, 0, o)),
        ),
        compiler_params=pltpu.CompilerParams(vmem_limit_bytes=VLIM),
        name="products",
    )(code, slot, own, low, high, out_grad)
    got = lax.all_to_all(sent, "ctx", 0, 0, tiled=True)

    rows = blocks * ch
    pad = HOPS * ch
    reply = pl.pallas_call(
        long_kernel,
        out_shape=jax.ShapeDtypeStruct((peers, 2, ch, tokens + LANES), BF16),
        in_specs=[smem(), vmem(), vmem(), vmem()],
        out_specs=vmem(),
        scratch_shapes=[
            VMEM((rows, BLK), BF16),
            VMEM((rows, BLK), BF16),
            VMEM((rows + pad, BLK), BF16),
            VMEM((rows + pad, BLK), BF16),
            VMEM((rows + pad, BLK), BF16),
            VMEM((rows, BLK), jnp.int32),
            VMEM((rows, BLK), jnp.int32),
            VMEM((rows, BLK), BF16),
            VMEM((rows, BLK), BF16),
            VMEM((rows, BLK), BF16),
            VMEM((BLK, rows), BF16),
            VMEM((BLK, rows), BF16),
            VMEM((BLK, rows), BF16),
            VMEM((rows, BLK), F32),
            VMEM((rows, BLK), F32),
            VMEM((BLK, BLK * (HOPS + 1)), F32),
            VMEM((2 * ch, LANES), F32),
        ],
        compiler_params=pltpu.CompilerParams(vmem_limit_bytes=VLIM),
        name="long_filter",
    )(table, got, fwd_band, bwd_band)
    back = lax.all_to_all(reply, "ctx", 0, 0, tiled=True)

    sums = back[:, :, :, tokens:].astype(F32).reshape(peers, 2 * ch, LANES)
    count = BLK * (HOPS + 1) // LANES
    tap_sum = sums[:, :count].reshape(filters, peers // filters, count * LANES).sum(axis=1)
    skip_total = (sums[:, count, :ch] + sums[:, count + 1, :ch]).reshape(channels)
    other = lax.ppermute(tap_sum, "ch", [(0, 1), (1, 0)])

    out_y, grads = pl.pallas_call(
        finish_kernel,
        out_shape=(
            jax.ShapeDtypeStruct((tokens, channels), BF16),
            jax.ShapeDtypeStruct((streams, tokens, channels), BF16),
        ),
        grid_spec=pltpu.PrefetchScalarGridSpec(
            num_scalar_prefetch=2,
            grid=(ROWS,),
            in_specs=row_specs()
            + [
                pl.BlockSpec((1, channels), lambda o, code, slot: (0, 0)),
                pl.BlockSpec((peers, 2, ch, row_len), lambda o, code, slot: (0, 0, 0, o)),
            ],
            out_specs=(
                pl.BlockSpec((row_len, channels), lambda o, code, slot: (o, 0)),
                pl.BlockSpec((streams, row_len, channels), lambda o, code, slot: (0, o, 0)),
            ),
        ),
        compiler_params=pltpu.CompilerParams(vmem_limit_bytes=VLIM),
        name="finish",
    )(code, slot, own, low, high, out_grad, skip_gain[None], back)

    seq_total = tokens * peers
    chan_total = channels * lax.axis_size("ch")
    tap_total = (tap_sum + other)[:, ::-1][:, :tap_count]
    grad_taps = tap_total / math.sqrt(seq_total * chan_total / filters)
    grad_skip = skip_total / math.sqrt(seq_total)
    return (out_y, grads.transpose(1, 0, 2), grad_taps, grad_skip)


def solution(mesh):
    return jax.shard_map(
        on_device,
        mesh=mesh,
        in_specs=(P("ctx", None, None, "ch"), P(), P(), P(), P("ch"), P("ctx", "ch")),
        out_specs=(P("ctx", "ch"), P("ctx", None, "ch"), P(), P("ch")),
        check_vma=False,
    )
```

```python
import functools
import math

import jax
import jax.numpy as jnp
from jax import lax
from jax.experimental import pallas as pl
from jax.experimental.pallas import tpu as pltpu
from jax.sharding import PartitionSpec as P

BF16 = jnp.bfloat16
F32 = jnp.float32
SMEM = pltpu.SMEM
VMEM = pltpu.VMEM

BLK = 256
HOPS = 8
SLOTS = 6
ROWS = 4
LANES = 128
TAP_ROWS = 17
VLIM = 56 * 1024 * 1024


def smem():
    return pl.BlockSpec(memory_space=SMEM)


def vmem():
    return pl.BlockSpec(memory_space=VMEM)


def choose_kernel(
    cycle, me_ref, target_ref, own_ref, up_ref, down_ref, up_kv_ref, down_kv_ref,
    code_ref, slot_ref, sems,
):
    me = me_ref[0]
    below = lax.rem(me + cycle - 1, cycle)
    above = lax.rem(me + 1, cycle)
    up_slot = jnp.int32(0)
    down_slot = jnp.int32(0)
    for k in range(SLOTS):
        shard = target_ref[0, me * SLOTS + k]
        up_slot = jnp.where(shard == above, k, up_slot)
        down_slot = jnp.where(shard == below, k, down_slot)
    copies = []
    for n, (slot, first, later) in enumerate(
        ((up_slot, up_ref, up_kv_ref), (down_slot, down_ref, down_kv_ref))
    ):
        copies.append(
            (
                pltpu.make_async_copy(own_ref.at[slot, 0], first.at[0], sems.at[2 * n]),
                pltpu.make_async_copy(own_ref.at[slot, pl.ds(1, 2)], later, sems.at[2 * n + 1]),
            )
        )
    for one, two in copies:
        two.start()
        one.start()
    for o in range(ROWS):
        code_ref[o] = 0
        slot_ref[o] = 0
    for k in range(SLOTS):
        shard = target_ref[0, me * SLOTS + k]
        offset = target_ref[1, me * SLOTS + k]

        @pl.when(shard == me)
        def _():
            slot_ref[offset] = k

        for owner, code in ((below, 1), (above, 2)):
            their_shard = target_ref[0, owner * SLOTS + k]
            their_offset = target_ref[1, owner * SLOTS + k]

            @pl.when(their_shard == me)
            def _():
                code_ref[their_offset] = code

    for (one, two), first, later in zip(copies, (up_ref, down_ref), (up_kv_ref, down_kv_ref)):
        two.wait()
        first[1] = round_mul(later[0], later[1])
        one.wait()


def tables_kernel(docs, length_ref, taps_ref, table_ref, fwd_ref, bwd_ref):
    def one_doc(d, start):
        end = start + length_ref[d]
        table_ref[3, d] = start
        table_ref[4, d] = end

        def heads(b, carry):
            table_ref[0, b] = b - lax.shift_right_logical(start, 8)
            table_ref[1, b] = jnp.minimum(end - BLK * b, BLK)
            return carry

        def tails(b, carry):
            table_ref[2, b] = jnp.maximum(start - BLK * b, 0)
            return carry

        lax.fori_loop(
            lax.shift_right_logical(start + BLK - 1, 8),
            lax.shift_right_logical(end + BLK - 1, 8),
            heads,
            0,
        )
        lax.fori_loop(
            lax.shift_right_logical(start, 8), lax.shift_right_logical(end, 8), tails, 0
        )
        return end

    lax.fori_loop(0, docs, one_doc, jnp.int32(0))
    width = BLK * (HOPS + 2)
    part = 32
    for r in range(BLK // part):
        rows = jnp.broadcast_to(taps_ref[...], (part, width))
        rows = pltpu.roll(rows, part * r, 1, stride=1, stride_axis=0)
        for delta in range(HOPS + 1):
            at = BLK * (HOPS - delta) + part * r
            fwd_ref[at : at + part, :] = rows[:, BLK * (delta + 1) : BLK * (delta + 2)].astype(BF16)
    for delta in range(HOPS + 1):
        at = BLK * (HOPS - delta)
        bwd_ref[BLK * delta : BLK * (delta + 1), :] = fwd_ref[at : at + BLK, :].T


def round_mul(a, b):
    return (a.astype(F32) * b.astype(F32)).astype(BF16)


def make_kernel(code_ref, slot_ref, own_ref, low_ref, high_ref, grad_ref, sent_ref):
    code = code_ref[pl.program_id(0)]

    def emit(query, product):
        grad_mid = round_mul(grad_ref[...], query)
        peers, _, chans, toks = sent_ref.shape
        sent_ref[:, 0] = product.T.reshape(peers, chans, toks)
        sent_ref[:, 1] = grad_mid.T.reshape(peers, chans, toks)

    pl.when(code == 0)(lambda: emit(own_ref[0, 0], round_mul(own_ref[0, 1], own_ref[0, 2])))
    pl.when(code == 1)(lambda: emit(low_ref[0], low_ref[1]))
    pl.when(code == 2)(lambda: emit(high_ref[0], high_ref[1]))


def place_of(b, peers):
    src = jnp.where(b < peers, b, 2 * peers - 1 - b)
    lane = pl.multiple_of(jnp.where(b < peers, 0, BLK), BLK)
    return src, lane


def long_kernel(
    table_ref, got_ref, fwd_ref, bwd_ref, out_ref,
    x_all, z_all, x_tail, z_head, reach, head_end, tail_start,
    xd, ze, xe, flip_all, flip_tail, flip_doc, conv, back, pairs, extra,
):
    peers = got_ref.shape[0]
    ch = got_ref.shape[2]
    blocks = 2 * peers
    docs = blocks
    rows = blocks * ch
    pad = HOPS * ch
    lane = lax.broadcasted_iota(jnp.int32, (ch, BLK), 1)
    zero = jnp.zeros((), BF16)

    x_tail[0:pad, :] = jnp.zeros((pad, BLK), BF16)
    z_head[rows : rows + pad, :] = jnp.zeros((pad, BLK), BF16)
    reach[rows : rows + pad, :] = jnp.full((pad, BLK), -1, BF16)

    def spread(b, total):
        src, at_lane = place_of(b, peers)
        at = pl.multiple_of(b * ch, ch)
        x = got_ref[src, 0, :, pl.ds(at_lane, BLK)]
        z = got_ref[src, 1, :, pl.ds(at_lane, BLK)]
        x_all[pl.ds(at, ch), :] = x
        z_all[pl.ds(at, ch), :] = z
        first, end, tail = table_ref[0, b], table_ref[1, b], table_ref[2, b]
        x_f, z_f = x.astype(F32), z.astype(F32)
        x_tail[pl.ds(at + pad, ch), :] = jnp.where(lane >= tail, x_f, 0).astype(BF16)
        z_head[pl.ds(at, ch), :] = jnp.where(lane < end, z_f, 0).astype(BF16)
        reach[pl.ds(at, ch), :] = jnp.full((ch, BLK), first.astype(F32)).astype(BF16)
        head_end[pl.ds(at, ch), :] = jnp.full((ch, BLK), end, jnp.int32)
        tail_start[pl.ds(at, ch), :] = jnp.full((ch, BLK), tail, jnp.int32)
        return total + x_f * z_f

    skip = lax.fori_loop(0, blocks, spread, jnp.zeros((ch, BLK), F32))

    def doc_parts(d):
        start, end = table_ref[3, d], table_ref[4, d]
        end_block = lax.shift_right_logical(end - 1, 8)
        end_at = jnp.bitwise_and(end, BLK - 1)
        end_from = jnp.maximum(start - BLK * end_block, 0)
        start_block = lax.shift_right_logical(start, 8)
        start_at = jnp.bitwise_and(start, BLK - 1)
        start_at = jnp.where(start_at == 0, BLK, start_at)
        start_to = end - BLK * start_block
        return end_block, end_from, end_at, start_block, start_at, start_to

    def spread_docs(d, carry):
        end_block, end_from, end_at, start_block, start_at, start_to = doc_parts(d)
        at = pl.multiple_of(d * ch, ch)
        at_end = pl.multiple_of(end_block * ch, ch)
        at_start = pl.multiple_of(start_block * ch, ch)
        ends = (lane >= end_from) & (lane < end_at)
        begins = (lane >= start_at) & (lane < start_to)
        x = x_all[pl.ds(at_end, ch), :].astype(F32)
        x2 = x_all[pl.ds(at_start, ch), :].astype(F32)
        z2 = z_all[pl.ds(at_start, ch), :].astype(F32)
        xd[pl.ds(at, ch), :] = jnp.where(ends, x, 0).astype(BF16)
        ze[pl.ds(at, ch), :] = jnp.where(begins, z2, 0).astype(BF16)
        xe[pl.ds(at, ch), :] = jnp.where(begins, x2, 0).astype(BF16)
        return carry

    lax.fori_loop(0, docs, spread_docs, 0)

    r_id = lax.broadcasted_iota(jnp.int32, (BLK, BLK), 0)
    c_id = lax.broadcasted_iota(jnp.int32, (BLK, BLK), 1)
    anti = jnp.where(r_id + c_id == BLK - 1, 1.0, 0.0).astype(BF16)
    step = 256
    steps = rows // step

    def flips(c, carry):
        at = pl.multiple_of(c * step, step)
        for src, skew, dst in ((x_all, 0, flip_all), (x_tail, pad, flip_tail), (xe, 0, flip_doc)):
            dst[:, pl.ds(at, step)] = lax.dot_general(
                anti, src[pl.ds(at + skew, step), :], (((1,), (1,)), ((), ())),
                preferred_element_type=F32,
            ).astype(BF16)
        return carry

    lax.fori_loop(0, steps, flips, 0)
    pairs[...] = jnp.zeros_like(pairs)
    wide = lax.broadcasted_iota(jnp.int32, (step, BLK), 1)
    far = HOPS * BLK

    def dot(a, b):
        return jnp.dot(a, b, preferred_element_type=F32)

    def chunk(c, carry):
        at = pl.multiple_of(c * step, step)
        here = reach[pl.ds(at, step), :]
        xs = []
        for delta in range(HOPS, -1, -1):
            x = x_tail[pl.ds(at + ch * (HOPS - delta), step), :]
            xs.append(jnp.where(here >= delta, x, zero) if delta else x)
        x_far = jnp.concatenate(xs[:-1], axis=1)
        far_part = dot(x_far, fwd_ref[0:far, :])
        far_part = jnp.where(wide < head_end[pl.ds(at, step), :], far_part, 0.0)
        conv[pl.ds(at, step), :] = far_part + dot(xs[-1], fwd_ref[far:, :])
        zs = []
        for delta in range(HOPS + 1):
            z = z_head[pl.ds(at + ch * delta, step), :]
            there = reach[pl.ds(at + ch * delta, step), :]
            zs.append(jnp.where(there >= delta, z, zero) if delta else z)
        z_far = jnp.concatenate(zs[1:], axis=1)
        far_part = dot(z_far, bwd_ref[BLK:, :])
        far_part = jnp.where(wide >= tail_start[pl.ds(at, step), :], far_part, 0.0)
        back[pl.ds(at, step), :] = far_part + dot(zs[0], bwd_ref[0:BLK, :])
        pairs[:, BLK:] += dot(flip_tail[:, pl.ds(at, step)], z_far)
        pairs[:, 0:BLK] += dot(flip_all[:, pl.ds(at, step)], zs[0]) + dot(
            flip_doc[:, pl.ds(at, step)], ze[pl.ds(at, step), :]
        )
        return carry

    lax.fori_loop(0, steps, chunk, 0)

    def doc_chunk(c, carry):
        at = pl.multiple_of(c * step, step)
        y_end = dot(xd[pl.ds(at, step), :], fwd_ref[far:, :])
        y_start = dot(ze[pl.ds(at, step), :], bwd_ref[0:BLK, :])
        for i in range(step // ch):
            d = c * (step // ch) + i
            end_block, end_from, end_at, start_block, start_at, start_to = doc_parts(d)
            at_end = pl.multiple_of(end_block * ch, ch)
            at_start = pl.multiple_of(start_block * ch, ch)
            conv[pl.ds(at_end, ch), :] += jnp.where(
                lane < end_at, y_end[i * ch : (i + 1) * ch], 0.0
            )
            back[pl.ds(at_start, ch), :] += jnp.where(
                lane >= start_at, y_start[i * ch : (i + 1) * ch], 0.0
            )
        return carry

    lax.fori_loop(0, steps, doc_chunk, 0)

    def gather_out(b, carry):
        src, at_lane = place_of(b, peers)
        at = pl.multiple_of(b * ch, ch)
        out_ref[src, 0, :, pl.ds(at_lane, BLK)] = conv[pl.ds(at, ch), :].astype(BF16)
        out_ref[src, 1, :, pl.ds(at_lane, BLK)] = back[pl.ds(at, ch), :].astype(BF16)
        return carry

    lax.fori_loop(0, blocks, gather_out, 0)

    total = jnp.zeros((8, far + 2 * BLK), F32)
    for r in range(BLK // 8):
        band = jnp.concatenate([pairs[8 * r : 8 * (r + 1), :], jnp.zeros((8, BLK), F32)], axis=1)
        total = total + pltpu.roll(band, 8 * r + 1, 1, stride=1, stride_axis=0)
    lags = jnp.sum(total, axis=0, keepdims=True)
    extra[...] = jnp.zeros_like(extra)
    count = TAP_ROWS
    for r in range(count):
        extra[r : r + 1, :] = lags[:, BLK + LANES * r : BLK + LANES * (r + 1)]
    by_channel = jnp.sum(skip, axis=1, keepdims=True)
    e_row = lax.broadcasted_iota(jnp.int32, (ch, LANES), 0)
    e_col = lax.broadcasted_iota(jnp.int32, (ch, LANES), 1)
    skip_row = jnp.sum(jnp.where(e_row == e_col, by_channel, 0.0), axis=0, keepdims=True)
    high = skip_row.astype(BF16).astype(F32)
    extra[count : count + 1, :] = high
    extra[count + 1 : count + 2, :] = skip_row - high
    packed = extra[...].astype(BF16)
    for side in range(2):
        out_ref[:, side, :, 2 * BLK : 2 * BLK + LANES] = jnp.broadcast_to(
            packed[side * ch : (side + 1) * ch][None], (peers, ch, LANES)
        )


def finish_kernel(
    code_ref, slot_ref, own_ref, low_ref, high_ref, grad_ref,
    low_kv_ref, high_kv_ref, gain_ref, got_ref, y_ref, grads_ref,
):
    code = code_ref[pl.program_id(0)]

    def emit(query, key_in, value):
        peers, _, chans, toks = got_ref.shape
        width = peers * chans
        conv = got_ref[:, 0].reshape(width, toks).T.astype(F32)
        back = got_ref[:, 1].reshape(width, toks).T.astype(F32)
        query, key_in, value = (a.astype(F32) for a in (query, key_in, value))
        grad = grad_ref[...].astype(F32)
        gain = gain_ref[...]
        product = (key_in * value).astype(BF16).astype(F32)
        grad_mid = (grad * query).astype(BF16).astype(F32)
        mixed = conv + gain * product
        grad_x = back + gain * grad_mid
        y_ref[...] = (query * mixed).astype(BF16)
        grads_ref[0] = (grad * mixed).astype(BF16)
        grads_ref[1] = (grad_x * value).astype(BF16)
        grads_ref[2] = (grad_x * key_in).astype(BF16)

    pl.when(code == 0)(lambda: emit(own_ref[0, 0], own_ref[0, 1], own_ref[0, 2]))
    pl.when(code == 1)(lambda: emit(low_ref[0], low_kv_ref[0], low_kv_ref[1]))
    pl.when(code == 2)(lambda: emit(high_ref[0], high_kv_ref[0], high_kv_ref[1]))


def totals_kernel(tap_scale, skip_scale, part_ref, taps_ref, skip_ref):
    filters, count, lanes = taps_ref.shape
    peers, _, ch, _ = part_ref.shape
    group = peers // filters
    for f in range(filters):
        part = part_ref[f * group : (f + 1) * group].astype(F32)
        total = jnp.sum(part, axis=0) * tap_scale
        taps_ref[f, 0:ch] = total[0]
        taps_ref[f, ch:] = total[1, 0 : count - ch]
    side = part_ref[:, 1].astype(F32)
    at = count - ch
    skip_ref[...] = (side[:, at, :] + side[:, at + 1, :]) * skip_scale


def shifted(array, axis, by):
    length = lax.axis_size(axis)
    return lax.ppermute(array, axis, [(i, (i + by) % length) for i in range(length)])


def on_device(rollout_rows, pack_targets, doc_lengths, filter_taps, skip_gain, out_grad):
    peers = lax.axis_size("ctx")
    index = lax.axis_index("ctx").astype(jnp.int32)
    slots, row_len, streams, channels = rollout_rows.shape
    tokens = out_grad.shape[0]
    filters, tap_count = filter_taps.shape
    docs = doc_lengths.shape[0]
    ch = channels // peers
    blocks = 2 * peers
    own = rollout_rows.transpose(0, 2, 1, 3)
    half_shape = jax.ShapeDtypeStruct((2, row_len, channels), BF16)
    list_shape = jax.ShapeDtypeStruct((ROWS,), jnp.int32)
    up, down, up_kv, down_kv, code, slot = pl.pallas_call(
        functools.partial(choose_kernel, peers),
        out_shape=(half_shape,) * 4 + (list_shape,) * 2,
        in_specs=[smem(), smem(), pl.BlockSpec(memory_space=pl.ANY)],
        out_specs=(vmem(),) * 4 + (smem(),) * 2,
        scratch_shapes=[pltpu.SemaphoreType.DMA((4,))],
        compiler_params=pltpu.CompilerParams(vmem_limit_bytes=VLIM),
        name="choose",
    )(index[None], pack_targets.T, own)
    low = shifted(up, "ctx", 1)
    high = shifted(down, "ctx", -1)

    mine = lax.dynamic_index_in_dim(filter_taps, index // (peers // filters), 0, keepdims=True)
    mine = mine.astype(BF16).astype(F32)
    mine = jnp.pad(mine, [(0, 0), (BLK, BLK * (HOPS + 1) - tap_count)])
    band = jax.ShapeDtypeStruct((BLK * (HOPS + 1), BLK), BF16)
    table, fwd_band, bwd_band = pl.pallas_call(
        functools.partial(tables_kernel, docs),
        out_shape=(jax.ShapeDtypeStruct((8, docs), jnp.int32), band, band),
        in_specs=[smem(), vmem()],
        out_specs=(smem(), vmem(), vmem()),
        compiler_params=pltpu.CompilerParams(vmem_limit_bytes=VLIM),
        cost_estimate=pl.CostEstimate(flops=0, bytes_accessed=20_000_000, transcendentals=0),
        name="tables",
    )(doc_lengths, mine)

    def row_specs():
        return [
            pl.BlockSpec(
                (1, streams, row_len, channels), lambda o, code, slot: (slot[o], 0, 0, 0)
            ),
            pl.BlockSpec((2, row_len, channels), lambda o, code, slot: (0, 0, 0)),
            pl.BlockSpec((2, row_len, channels), lambda o, code, slot: (0, 0, 0)),
            pl.BlockSpec((row_len, channels), lambda o, code, slot: (o, 0)),
        ]

    sent = pl.pallas_call(
        make_kernel,
        out_shape=jax.ShapeDtypeStruct((peers, 2, ch, tokens), BF16),
        grid_spec=pltpu.PrefetchScalarGridSpec(
            num_scalar_prefetch=2,
            grid=(ROWS,),
            in_specs=row_specs(),
            out_specs=pl.BlockSpec((peers, 2, ch, row_len), lambda o, code, slot: (0, 0, 0, o)),
        ),
        compiler_params=pltpu.CompilerParams(vmem_limit_bytes=VLIM),
        name="products",
    )(code, slot, own, low, high, out_grad)
    got = lax.all_to_all(sent, "ctx", 0, 0, tiled=True)
    up_kv, down_kv, got = lax.optimization_barrier((up_kv, down_kv, got))
    low_kv = shifted(up_kv, "ctx", 1)
    high_kv = shifted(down_kv, "ctx", -1)

    rows = blocks * ch
    pad = HOPS * ch
    reply = pl.pallas_call(
        long_kernel,
        out_shape=jax.ShapeDtypeStruct((peers, 2, ch, tokens + LANES), BF16),
        in_specs=[smem(), vmem(), vmem(), vmem()],
        out_specs=vmem(),
        scratch_shapes=[
            VMEM((rows, BLK), BF16),
            VMEM((rows, BLK), BF16),
            VMEM((rows + pad, BLK), BF16),
            VMEM((rows + pad, BLK), BF16),
            VMEM((rows + pad, BLK), BF16),
            VMEM((rows, BLK), jnp.int32),
            VMEM((rows, BLK), jnp.int32),
            VMEM((rows, BLK), BF16),
            VMEM((rows, BLK), BF16),
            VMEM((rows, BLK), BF16),
            VMEM((BLK, rows), BF16),
            VMEM((BLK, rows), BF16),
            VMEM((BLK, rows), BF16),
            VMEM((rows, BLK), F32),
            VMEM((rows, BLK), F32),
            VMEM((BLK, BLK * (HOPS + 1)), F32),
            VMEM((2 * ch, LANES), F32),
        ],
        compiler_params=pltpu.CompilerParams(vmem_limit_bytes=34 * 1024 * 1024),
        cost_estimate=pl.CostEstimate(
            flops=2 * 30 * rows * BLK * BLK, bytes_accessed=7_000_000, transcendentals=0
        ),
        name="long_filter",
    )(table, got, fwd_band, bwd_band)
    low_kv, high_kv, reply = lax.optimization_barrier((low_kv, high_kv, reply))
    back = lax.all_to_all(reply, "ctx", 0, 0, tiled=True)

    seq_total = tokens * peers
    chan_total = channels * lax.axis_size("ch")
    tap_sum, skip_sum = pl.pallas_call(
        functools.partial(
            totals_kernel,
            1.0 / math.sqrt(seq_total * chan_total / filters),
            1.0 / math.sqrt(seq_total),
        ),
        out_shape=(
            jax.ShapeDtypeStruct((filters, TAP_ROWS, LANES), F32),
            jax.ShapeDtypeStruct((peers, LANES), F32),
        ),
        grid=(1,),
        in_specs=[
            pl.BlockSpec((peers, 2, ch, LANES), lambda o: (0, 0, 0, tokens // LANES)),
        ],
        out_specs=(
            pl.BlockSpec((filters, TAP_ROWS, LANES), lambda o: (0, 0, 0)),
            pl.BlockSpec((peers, LANES), lambda o: (0, 0)),
        ),
        name="totals",
    )(back)
    other = lax.ppermute(tap_sum, "ch", [(0, 1), (1, 0)])

    out_y, grads = pl.pallas_call(
        finish_kernel,
        out_shape=(
            jax.ShapeDtypeStruct((tokens, channels), BF16),
            jax.ShapeDtypeStruct((streams, tokens, channels), BF16),
        ),
        grid_spec=pltpu.PrefetchScalarGridSpec(
            num_scalar_prefetch=2,
            grid=(ROWS,),
            in_specs=row_specs()
            + [
                pl.BlockSpec((2, row_len, channels), lambda o, code, slot: (0, 0, 0)),
                pl.BlockSpec((2, row_len, channels), lambda o, code, slot: (0, 0, 0)),
                pl.BlockSpec((1, channels), lambda o, code, slot: (0, 0)),
                pl.BlockSpec((peers, 2, ch, row_len), lambda o, code, slot: (0, 0, 0, o)),
            ],
            out_specs=(
                pl.BlockSpec((row_len, channels), lambda o, code, slot: (o, 0)),
                pl.BlockSpec((streams, row_len, channels), lambda o, code, slot: (0, o, 0)),
            ),
        ),
        compiler_params=pltpu.CompilerParams(vmem_limit_bytes=VLIM),
        name="finish",
    )(code, slot, own, low, high, out_grad, low_kv, high_kv, skip_gain[None], back)

    grad_taps = (tap_sum + other).reshape(filters, TAP_ROWS * LANES)[:, :tap_count]
    grad_skip = skip_sum[:, :ch].reshape(channels)
    return (out_y, grads.transpose(1, 0, 2), grad_taps, grad_skip)


def solution(mesh):
    return jax.shard_map(
        on_device,
        mesh=mesh,
        in_specs=(P("ctx", None, None, "ch"), P(), P(), P(), P("ch"), P("ctx", "ch")),
        out_specs=(P("ctx", "ch"), P("ctx", None, "ch"), P(), P("ch")),
        check_vma=False,
    )
```

```python
import functools
import math

import jax
import jax.numpy as jnp
from jax import lax
from jax.experimental import pallas as pl
from jax.experimental.pallas import tpu as pltpu
from jax.sharding import PartitionSpec as P

BF16 = jnp.bfloat16
F32 = jnp.float32
SMEM = pltpu.SMEM
VMEM = pltpu.VMEM

BLK = 256
HOPS = 8
SLOTS = 6
ROWS = 4
LANES = 128
WIDE = 256
GROUP = 32
TAP_ROWS = 17
VLIM = 56 * 1024 * 1024


def hbm():
    return pl.BlockSpec(memory_space=pltpu.HBM)


def smem():
    return pl.BlockSpec(memory_space=SMEM)


def vmem():
    return pl.BlockSpec(memory_space=VMEM)


def choose_kernel(
    cycle, me_ref, target_ref, own_ref, up_ref, down_ref, up_kv_ref, down_kv_ref,
    code_ref, slot_ref, sems,
):
    me = me_ref[0]
    below = lax.rem(me + cycle - 1, cycle)
    above = lax.rem(me + 1, cycle)
    up_slot = jnp.int32(0)
    down_slot = jnp.int32(0)
    for k in range(SLOTS):
        shard = target_ref[0, me * SLOTS + k]
        up_slot = jnp.where(shard == above, k, up_slot)
        down_slot = jnp.where(shard == below, k, down_slot)
    copies = []
    for n, (slot, first, later) in enumerate(
        ((up_slot, up_ref, up_kv_ref), (down_slot, down_ref, down_kv_ref))
    ):
        copies.append(
            (
                pltpu.make_async_copy(own_ref.at[slot, 0], first.at[0], sems.at[2 * n]),
                pltpu.make_async_copy(own_ref.at[slot, pl.ds(1, 2)], later, sems.at[2 * n + 1]),
            )
        )
    for one, two in copies:
        two.start()
        one.start()
    for o in range(ROWS):
        code_ref[o] = 0
        slot_ref[o] = 0
    for k in range(SLOTS):
        shard = target_ref[0, me * SLOTS + k]
        offset = target_ref[1, me * SLOTS + k]

        @pl.when(shard == me)
        def _():
            slot_ref[offset] = k

        for owner, code in ((below, 1), (above, 2)):
            their_shard = target_ref[0, owner * SLOTS + k]
            their_offset = target_ref[1, owner * SLOTS + k]

            @pl.when(their_shard == me)
            def _():
                code_ref[their_offset] = code

    for (one, two), first, later in zip(copies, (up_ref, down_ref), (up_kv_ref, down_kv_ref)):
        two.wait()
        first[1] = round_mul(later[0], later[1])
        one.wait()


def tables_kernel(docs, length_ref, table_ref, count_ref):
    def one_doc(d, start):
        end = start + length_ref[d]
        table_ref[3, d] = start
        table_ref[4, d] = end

        def heads(b, carry):
            table_ref[0, b] = b - lax.shift_right_logical(start, 8)
            table_ref[1, b] = jnp.minimum(end - BLK * b, BLK)
            return carry

        def tails(b, carry):
            table_ref[2, b] = jnp.maximum(start - BLK * b, 0)
            return carry

        lax.fori_loop(
            lax.shift_right_logical(start + BLK - 1, 8),
            lax.shift_right_logical(end + BLK - 1, 8),
            heads,
            0,
        )
        lax.fori_loop(
            lax.shift_right_logical(start, 8), lax.shift_right_logical(end, 8), tails, 0
        )
        return end

    lax.fori_loop(0, docs, one_doc, jnp.int32(0))

    for n in range(HOPS + 1):
        count_ref[n] = 0

    def count(b, carry):
        reach = table_ref[0, b]
        count_ref[reach] = count_ref[reach] + 1
        return carry

    lax.fori_loop(0, docs, count, 0)
    before = jnp.int32(0)
    for n in range(HOPS, -1, -1):
        these = count_ref[n]
        count_ref[n] = before
        before = before + these

    def place(b, carry):
        reach = table_ref[0, b]
        at = count_ref[reach]
        count_ref[reach] = at + 1
        table_ref[5, at] = b
        table_ref[6, b] = at
        table_ref[7, at] = reach
        return carry

    lax.fori_loop(0, docs, place, 0)


def make_bands(taps_ref, fwd_ref, bwd_ref):
    width = BLK * (HOPS + 2)
    part = 32
    for r in range(BLK // part):
        rows = jnp.broadcast_to(taps_ref[...], (part, width))
        rows = pltpu.roll(rows, part * r, 1, stride=1, stride_axis=0)
        for delta in range(HOPS + 1):
            at = BLK * (HOPS - delta) + part * r
            fwd_ref[at : at + part, :] = rows[:, BLK * (delta + 1) : BLK * (delta + 2)].astype(BF16)
    for delta in range(HOPS + 1):
        at = BLK * (HOPS - delta)
        bwd_ref[BLK * delta : BLK * (delta + 1), :] = fwd_ref[at : at + BLK, :].T


def round_mul(a, b):
    return (a.astype(F32) * b.astype(F32)).astype(BF16)


def write_row(sent_ref, lane, toks, read_product, read_grad_mid):
    peers, _, chans, _ = sent_ref.shape
    together = WIDE // chans
    for n in range(peers // together):
        lanes = slice(n * WIDE, (n + 1) * WIDE)
        to = slice(n * together, (n + 1) * together)
        for side, read in enumerate((read_product, read_grad_mid)):
            sent_ref[to, side, :, lane : lane + toks] = read(lanes).T.reshape(together, chans, toks)


def own_kernel(code_ref, slot_ref, own_ref, grad_ref, sent_ref, row, grad, sems):
    toks = row.shape[2]

    def copies(o):
        return (
            pltpu.make_async_copy(own_ref.at[slot_ref[o]], row.at[o], sems.at[o]),
            pltpu.make_async_copy(
                grad_ref.at[pl.ds(o * toks, toks)], grad.at[o], sems.at[ROWS + o]
            ),
        )

    for o in range(ROWS):
        for copy in copies(o):
            copy.start()
    for o in range(ROWS):
        for copy in copies(o):
            copy.wait()

        @pl.when(code_ref[o] == 0)
        def _():
            write_row(
                sent_ref,
                o * toks,
                toks,
                lambda c: round_mul(row[o, 1, :, c], row[o, 2, :, c]),
                lambda c: round_mul(grad[o, :, c], row[o, 0, :, c]),
            )


def guest_kernel(code_ref, low_ref, high_ref, grad_ref, part_ref, sent_ref, grad, ready, sems):
    del part_ref
    toks = low_ref.shape[1]
    guests = []
    for n, ref in enumerate((low_ref, high_ref)):
        at = jnp.int32(0)
        for o in range(ROWS):
            at = jnp.where(code_ref[o] == n + 1, o + 1, at)
        here = pl.ds(pl.multiple_of(jnp.maximum(at - 1, 0) * toks, toks), toks)
        copy_in = pltpu.make_async_copy(grad_ref.at[here], grad.at[n], sems.at[n])
        copy_out = pltpu.make_async_copy(
            ready.at[n], sent_ref.at[:, :, :, here], sems.at[2 + n]
        )
        guests.append((n, ref, at > 0, copy_in, copy_out))
    for n, ref, live, copy_in, copy_out in guests:
        pl.when(live)(copy_in.start)
    for n, ref, live, copy_in, copy_out in guests:

        @pl.when(live)
        def _():
            copy_in.wait()
            write_row(
                ready.at[n],
                0,
                toks,
                lambda c: ref[1, :, c],
                lambda c: round_mul(grad[n, :, c], ref[0, :, c]),
            )
            copy_out.start()

    for n, ref, live, copy_in, copy_out in guests:
        pl.when(live)(copy_out.wait)


def place_of(b, peers):
    src = jnp.where(b < peers, b, 2 * peers - 1 - b)
    lane = pl.multiple_of(jnp.where(b < peers, 0, BLK), BLK)
    return src, lane


def dot(a, b):
    return jnp.dot(a, b, preferred_element_type=F32)


def long_kernel(
    me_ref, table_ref, got_ref, taps_ref, out_ref,
    fwd_ref, bwd_ref, x_all, z_all, x_tail, z_head, xd, zd, ze, turned, doc_near, doc_back,
    near, far_sum, back_near, back_far, pairs, extra,
):
    peers = got_ref.shape[0]
    ch = got_ref.shape[2]
    blocks = 2 * peers
    docs = blocks
    rows = blocks * ch
    pad = HOPS * ch
    far = HOPS * BLK
    lane = lax.broadcasted_iota(jnp.int32, (ch, BLK), 1)

    make_bands(taps_ref, fwd_ref, bwd_ref)
    x_tail[0:pad, :] = jnp.zeros((pad, BLK), BF16)
    back_far[...] = jnp.zeros_like(back_far)
    far_sum[...] = jnp.zeros_like(far_sum)
    pairs[...] = jnp.zeros_like(pairs)

    def spread(k, total):
        b = table_ref[5, k]
        src, at_lane = place_of(b, peers)
        at = pl.multiple_of(b * ch, ch)
        x = got_ref[src, 0, :, pl.ds(at_lane, BLK)]
        z = got_ref[src, 1, :, pl.ds(at_lane, BLK)]
        x_all[pl.ds(at, ch), :] = x
        z_all[pl.ds(at, ch), :] = z
        end, tail = table_ref[1, b], table_ref[2, b]
        x_f, z_f = x.astype(F32), z.astype(F32)
        x_tail[pl.ds(at + pad, ch), :] = jnp.where(lane >= tail, x_f, 0).astype(BF16)
        z_head[pl.ds(pl.multiple_of(k * ch, ch), ch), :] = jnp.where(lane < end, z_f, 0).astype(BF16)
        return total + x_f * z_f

    skip = lax.fori_loop(0, blocks, spread, jnp.zeros((ch, BLK), F32), unroll=4)

    def doc_parts(d):
        start, end = table_ref[3, d], table_ref[4, d]
        end_block = lax.shift_right_logical(end - 1, 8)
        end_at = jnp.bitwise_and(end, BLK - 1)
        end_from = jnp.maximum(start - BLK * end_block, 0)
        start_block = lax.shift_right_logical(start, 8)
        start_at = jnp.bitwise_and(start, BLK - 1)
        start_at = jnp.where(start_at == 0, BLK, start_at)
        start_to = end - BLK * start_block
        return end_block, end_from, end_at, start_block, start_at, start_to

    def spread_docs(d, carry):
        end_block, end_from, end_at, start_block, start_at, start_to = doc_parts(d)
        at = pl.multiple_of(d * ch, ch)
        at_end = pl.multiple_of(end_block * ch, ch)
        at_start = pl.multiple_of(start_block * ch, ch)
        ends = (lane >= end_from) & (lane < end_at)
        begins = (lane >= start_at) & (lane < start_to)
        x = x_all[pl.ds(at_end, ch), :].astype(F32)
        z = z_all[pl.ds(at_end, ch), :].astype(F32)
        z2 = z_all[pl.ds(at_start, ch), :].astype(F32)
        xd[pl.ds(at, ch), :] = jnp.where(ends, x, 0).astype(BF16)
        zd[pl.ds(at, ch), :] = jnp.where(ends, z, 0).astype(BF16)
        ze[pl.ds(at, ch), :] = jnp.where(begins, z2, 0).astype(BF16)
        return carry

    lax.fori_loop(0, docs, spread_docs, 0, unroll=4)

    step = 256
    first_fwd = fwd_ref.at[far : far + BLK, :]
    first_bwd = bwd_ref.at[0:BLK, :]

    def inner(c, carry):
        at = pl.multiple_of(c * step, step)
        here = pl.ds(at, step)
        z = z_head[here, :]
        x = jnp.concatenate([x_tail[pl.ds(at + pad, step), :], xd[here, :]], axis=0)
        ahead = dot(x, first_fwd[...])
        near[here, :] = ahead[:step]
        doc_near[here, :] = ahead[step:]
        behind = dot(jnp.concatenate([z, ze[here, :]], axis=0), first_bwd[...])
        back_near[here, :] = behind[:step]
        doc_back[here, :] = behind[step:]
        turned[:, here] = z.T
        pairs[:, far:] += dot(jnp.concatenate([z_all[here, :].T, zd[here, :].T], axis=1), x)
        return carry

    lax.fori_loop(0, rows // step, inner, 0)

    def add_docs(d, carry):
        end_block, end_from, end_at, start_block, start_at, start_to = doc_parts(d)
        here = pl.ds(pl.multiple_of(d * ch, ch), ch)
        at_end = pl.multiple_of(end_block * ch, ch)
        at_start = pl.multiple_of(table_ref[6, start_block] * ch, ch)
        near[pl.ds(at_end, ch), :] += jnp.where(lane < end_at, doc_near[here, :], 0.0)
        back_near[pl.ds(at_start, ch), :] += jnp.where(lane >= start_at, doc_back[here, :], 0.0)
        return carry

    lax.fori_loop(0, docs, add_docs, 0, unroll=4)

    wide = GROUP * ch
    zero = jnp.zeros((), BF16)

    def outer(c, carry):
        at = pl.multiple_of(c * wide, wide)
        here = pl.ds(at, wide)

        def one_lag(delta, carry):
            tiles, targets, live = [], [], []
            for i in range(GROUP):
                k = c * GROUP + i
                target = pl.multiple_of((table_ref[5, k] + HOPS - delta) * ch, ch)
                inside = table_ref[7, k] >= delta
                tiles.append(jnp.where(inside, x_tail[pl.ds(target, ch), :], zero))
                targets.append(target)
                live.append(inside)
            x = jnp.concatenate(tiles, axis=0)
            fwd_at = pl.multiple_of((HOPS - delta) * BLK, BLK)
            bwd_at = pl.multiple_of(delta * BLK, BLK)
            far_sum[here, :] += dot(x, fwd_ref[pl.ds(fwd_at, BLK), :])
            pairs[:, pl.ds(fwd_at, BLK)] += dot(turned[:, here], x)
            y = dot(z_head[here, :], bwd_ref[pl.ds(bwd_at, BLK), :])
            for i in range(GROUP):
                back_far[pl.ds(targets[i], ch), :] += jnp.where(
                    live[i], y[i * ch : (i + 1) * ch], 0.0
                )
            return carry

        lax.fori_loop(1, table_ref[7, c * GROUP] + 1, one_lag, 0)
        return carry

    lax.fori_loop(0, blocks // GROUP, outer, 0)

    def gather_out(k, carry):
        b = table_ref[5, k]
        src, at_lane = place_of(b, peers)
        here = pl.ds(pl.multiple_of(k * ch, ch), ch)
        at = pl.multiple_of(b * ch, ch)
        ahead = jnp.where(lane < table_ref[1, b], far_sum[here, :], 0.0)
        behind = jnp.where(lane >= table_ref[2, b], back_far[pl.ds(at + pad, ch), :], 0.0)
        out_ref[src, 0, :, pl.ds(at_lane, BLK)] = (near[pl.ds(at, ch), :] + ahead).astype(BF16)
        out_ref[src, 1, :, pl.ds(at_lane, BLK)] = (back_near[here, :] + behind).astype(BF16)
        return carry

    lax.fori_loop(0, blocks, gather_out, 0, unroll=4)

    total = jnp.zeros((8, far + 2 * BLK), F32)
    for r in range(BLK // 8):
        band = jnp.concatenate([pairs[8 * r : 8 * (r + 1), :], jnp.zeros((8, BLK), F32)], axis=1)
        total = total + pltpu.roll(band, BLK - 8 - 8 * r, 1)
    lags = total[7:8]
    for r in range(7):
        lags = lags + pltpu.roll(total[r : r + 1], 7 - r, 1)
    extra[...] = jnp.zeros_like(extra)
    count = TAP_ROWS
    for r in range(count):
        at = far + BLK - LANES * (r + 1)
        extra[r : r + 1, :] = lags[:, at : at + LANES]
    r_id = lax.broadcasted_iota(jnp.int32, (LANES, LANES), 0)
    c_id = lax.broadcasted_iota(jnp.int32, (LANES, LANES), 1)
    anti = jnp.where(r_id + c_id == LANES - 1, 1.0, 0.0).astype(BF16)
    extra[...] = dot(extra[...].astype(BF16), anti)

    by_channel = jnp.sum(skip, axis=1, keepdims=True)
    e_row = lax.broadcasted_iota(jnp.int32, (ch, LANES), 0)
    e_col = lax.broadcasted_iota(jnp.int32, (ch, LANES), 1)
    mine = e_row + ch * lax.rem(me_ref[0], LANES // ch) == e_col
    skip_row = jnp.sum(jnp.where(mine, by_channel, 0.0), axis=0, keepdims=True)
    high = skip_row.astype(BF16).astype(F32)
    extra[count : count + 1, :] = high
    extra[count + 1 : count + 2, :] = skip_row - high
    packed = extra[...].astype(BF16)
    for side in range(2):
        out_ref[:, side, :, 2 * BLK : 2 * BLK + LANES] = jnp.broadcast_to(
            packed[side * ch : (side + 1) * ch][None], (peers, ch, LANES)
        )


def finish_kernel(
    code_ref, slot_ref, gain_ref, own_ref, low_ref, high_ref, grad_ref,
    low_kv_ref, high_kv_ref, got_ref, y_ref, grads_ref,
    row, grad, got, y_row, grads_row, in_sems, out_sems,
):
    _, peers, _, chans, toks = got.shape

    def here(o):
        return pl.ds(o * toks, toks)

    def fetch(o, act):
        code = code_ref[o]

        @pl.when(code == 0)
        def _():
            act(pltpu.make_async_copy(own_ref.at[slot_ref[o]], row.at[o], in_sems.at[o, 0]))

        for n, first, later in ((1, low_ref, low_kv_ref), (2, high_ref, high_kv_ref)):

            @pl.when(code == n)
            def _():
                act(pltpu.make_async_copy(first.at[0], row.at[o, 0], in_sems.at[o, 0]))
                act(pltpu.make_async_copy(later, row.at[o, pl.ds(1, 2)], in_sems.at[o, 1]))

        act(pltpu.make_async_copy(grad_ref.at[here(o)], grad.at[o], in_sems.at[o, 2]))
        act(pltpu.make_async_copy(got_ref.at[:, :, :, here(o)], got.at[o], in_sems.at[o, 3]))

    def results(o, act):
        act(pltpu.make_async_copy(y_row.at[o], y_ref.at[here(o)], out_sems.at[o, 0]))
        for n in range(3):
            act(
                pltpu.make_async_copy(
                    grads_row.at[o, n], grads_ref.at[n, here(o)], out_sems.at[o, 1 + n]
                )
            )

    together = WIDE // chans
    for o in range(ROWS):
        fetch(o, lambda copy: copy.start())
    for o in range(ROWS):
        fetch(o, lambda copy: copy.wait())
        for n in range(peers // together):
            lanes = slice(n * WIDE, (n + 1) * WIDE)
            of = slice(n * together, (n + 1) * together)
            conv = got[o, of, 0].reshape(WIDE, toks).T.astype(F32)
            back = got[o, of, 1].reshape(WIDE, toks).T.astype(F32)
            query, key_in, value = (row[o, s, :, lanes].astype(F32) for s in range(3))
            out_grad = grad[o, :, lanes].astype(F32)
            gain = gain_ref[:, lanes]
            product = (key_in * value).astype(BF16).astype(F32)
            grad_mid = (out_grad * query).astype(BF16).astype(F32)
            mixed = conv + gain * product
            grad_x = back + gain * grad_mid
            y_row[o, :, lanes] = (query * mixed).astype(BF16)
            grads_row[o, 0, :, lanes] = (out_grad * mixed).astype(BF16)
            grads_row[o, 1, :, lanes] = (grad_x * value).astype(BF16)
            grads_row[o, 2, :, lanes] = (grad_x * key_in).astype(BF16)
        results(o, lambda copy: copy.start())
    for o in range(ROWS):
        results(o, lambda copy: copy.wait())


def totals_kernel(tap_scale, skip_scale, part_ref, taps_ref, skip_ref):
    filters = taps_ref.shape[0]
    peers, _, ch, lanes = part_ref.shape
    group = peers // filters
    for f in range(filters):
        part = part_ref[f * group : (f + 1) * group].astype(F32)
        total = jnp.sum(part, axis=0) * tap_scale
        for r in range(TAP_ROWS):
            row = total[r // ch, r % ch : r % ch + 1]
            taps_ref[f : f + 1, r * lanes : (r + 1) * lanes] = row
    at = TAP_ROWS - ch
    together = lanes // ch
    for r in range(peers // together):
        part = part_ref[r * together : (r + 1) * together, 1, :, :].astype(F32)
        total = jnp.sum(part, axis=0) * skip_scale
        skip_ref[r : r + 1, :] = total[at : at + 1] + total[at + 1 : at + 2]


def shifted(array, axis, by):
    length = lax.axis_size(axis)
    return lax.ppermute(array, axis, [(i, (i + by) % length) for i in range(length)])


def on_device(rollout_rows, pack_targets, doc_lengths, filter_taps, skip_gain, out_grad):
    peers = lax.axis_size("ctx")
    index = lax.axis_index("ctx").astype(jnp.int32)
    slots, row_len, streams, channels = rollout_rows.shape
    tokens = out_grad.shape[0]
    filters, tap_count = filter_taps.shape
    docs = doc_lengths.shape[0]
    ch = channels // peers
    blocks = 2 * peers
    own = rollout_rows.transpose(0, 2, 1, 3)
    half_shape = jax.ShapeDtypeStruct((2, row_len, channels), BF16)
    list_shape = jax.ShapeDtypeStruct((ROWS,), jnp.int32)
    up, down, up_kv, down_kv, code, slot = pl.pallas_call(
        functools.partial(choose_kernel, peers),
        out_shape=(half_shape,) * 4 + (list_shape,) * 2,
        in_specs=[smem(), smem(), hbm()],
        out_specs=(vmem(),) * 4 + (smem(),) * 2,
        scratch_shapes=[pltpu.SemaphoreType.DMA((4,))],
        compiler_params=pltpu.CompilerParams(vmem_limit_bytes=VLIM),
        name="choose",
    )(index[None], pack_targets.T, own)
    low = shifted(up, "ctx", 1)
    high = shifted(down, "ctx", -1)

    mine = lax.dynamic_index_in_dim(filter_taps, index // (peers // filters), 0, keepdims=True)
    mine = mine.astype(BF16).astype(F32)
    mine = jnp.pad(mine, [(0, 0), (BLK, BLK * (HOPS + 1) - tap_count)])
    table = pl.pallas_call(
        functools.partial(tables_kernel, docs),
        out_shape=jax.ShapeDtypeStruct((8, docs), jnp.int32),
        in_specs=[smem()],
        out_specs=smem(),
        scratch_shapes=[SMEM((HOPS + 1,), jnp.int32)],
        compiler_params=pltpu.CompilerParams(vmem_limit_bytes=4 * 1024 * 1024),
        cost_estimate=pl.CostEstimate(flops=0, bytes_accessed=20_000_000, transcendentals=0),
        name="tables",
    )(doc_lengths)

    sent_shape = jax.ShapeDtypeStruct((peers, 2, ch, tokens), BF16)
    row_buffers = [
        VMEM((ROWS, streams, row_len, channels), BF16),
        VMEM((ROWS, row_len, channels), BF16),
    ]
    part = pl.pallas_call(
        own_kernel,
        out_shape=sent_shape,
        in_specs=[smem(), smem(), hbm(), hbm()],
        out_specs=vmem(),
        scratch_shapes=row_buffers + [pltpu.SemaphoreType.DMA((2 * ROWS,))],
        compiler_params=pltpu.CompilerParams(vmem_limit_bytes=VLIM),
        cost_estimate=pl.CostEstimate(flops=0, bytes_accessed=20_000_000, transcendentals=0),
        name="own_products",
    )(code, slot, own, out_grad)
    sent = pl.pallas_call(
        guest_kernel,
        out_shape=sent_shape,
        in_specs=[smem(), vmem(), vmem(), hbm(), hbm()],
        out_specs=hbm(),
        scratch_shapes=[
            VMEM((2, row_len, channels), BF16),
            VMEM((2, peers, 2, ch, row_len), BF16),
            pltpu.SemaphoreType.DMA((4,)),
        ],
        input_output_aliases={4: 0},
        compiler_params=pltpu.CompilerParams(vmem_limit_bytes=VLIM),
        name="guest_products",
    )(code, low, high, out_grad, part)
    got = lax.all_to_all(sent, "ctx", 0, 0, tiled=True)
    up_kv, down_kv, got = lax.optimization_barrier((up_kv, down_kv, got))
    low_kv = shifted(up_kv, "ctx", 1)
    high_kv = shifted(down_kv, "ctx", -1)

    rows = blocks * ch
    pad = HOPS * ch
    reply = pl.pallas_call(
        long_kernel,
        out_shape=jax.ShapeDtypeStruct((peers, 2, ch, tokens + LANES), BF16),
        in_specs=[smem(), smem(), vmem(), vmem()],
        out_specs=vmem(),
        scratch_shapes=[
            VMEM((BLK * (HOPS + 1), BLK), BF16),
            VMEM((BLK * (HOPS + 1), BLK), BF16),
            VMEM((rows, BLK), BF16),
            VMEM((rows, BLK), BF16),
            VMEM((rows + pad, BLK), BF16),
            VMEM((rows, BLK), BF16),
            VMEM((rows, BLK), BF16),
            VMEM((rows, BLK), BF16),
            VMEM((rows, BLK), BF16),
            VMEM((BLK, rows), BF16),
            VMEM((rows, BLK), F32),
            VMEM((rows, BLK), F32),
            VMEM((rows, BLK), F32),
            VMEM((rows, BLK), F32),
            VMEM((rows, BLK), F32),
            VMEM((rows + pad, BLK), F32),
            VMEM((BLK, BLK * (HOPS + 1)), F32),
            VMEM((2 * ch, LANES), F32),
        ],
        compiler_params=pltpu.CompilerParams(vmem_limit_bytes=32 * 1024 * 1024),
        cost_estimate=pl.CostEstimate(
            flops=2 * 30 * rows * BLK * BLK, bytes_accessed=7_000_000, transcendentals=0
        ),
        name="long_filter",
    )(index[None], table, got, mine)
    low_kv, high_kv, reply = lax.optimization_barrier((low_kv, high_kv, reply))
    back = lax.all_to_all(reply, "ctx", 0, 0, tiled=True)

    seq_total = tokens * peers
    chan_total = channels * lax.axis_size("ch")
    tap_sum, skip_sum = pl.pallas_call(
        functools.partial(
            totals_kernel,
            1.0 / math.sqrt(seq_total * chan_total / filters),
            1.0 / math.sqrt(seq_total),
        ),
        out_shape=(
            jax.ShapeDtypeStruct((filters, TAP_ROWS * LANES), F32),
            jax.ShapeDtypeStruct((channels // LANES, LANES), F32),
        ),
        grid=(1,),
        in_specs=[
            pl.BlockSpec((peers, 2, ch, LANES), lambda o: (0, 0, 0, tokens // LANES)),
        ],
        out_specs=(
            pl.BlockSpec((filters, TAP_ROWS * LANES), lambda o: (0, 0)),
            pl.BlockSpec((channels // LANES, LANES), lambda o: (0, 0)),
        ),
        name="totals",
    )(back)
    other = lax.ppermute(tap_sum, "ch", [(0, 1), (1, 0)])

    out_y, grads = pl.pallas_call(
        finish_kernel,
        out_shape=(
            jax.ShapeDtypeStruct((tokens, channels), BF16),
            jax.ShapeDtypeStruct((streams, tokens, channels), BF16),
        ),
        in_specs=[smem(), smem(), vmem()] + [hbm()] * 7,
        out_specs=(hbm(), hbm()),
        scratch_shapes=row_buffers
        + [
            VMEM((ROWS, peers, 2, ch, row_len), BF16),
            VMEM((ROWS, row_len, channels), BF16),
            VMEM((ROWS, streams, row_len, channels), BF16),
            pltpu.SemaphoreType.DMA((ROWS, 4)),
            pltpu.SemaphoreType.DMA((ROWS, 4)),
        ],
        compiler_params=pltpu.CompilerParams(vmem_limit_bytes=VLIM),
        name="finish",
    )(code, slot, skip_gain[None], own, low, high, out_grad, low_kv, high_kv, back)

    grad_taps = (tap_sum + other)[:, :tap_count]
    grad_skip = skip_sum.reshape(channels)
    return (out_y, grads.transpose(1, 0, 2), grad_taps, grad_skip)


def solution(mesh):
    return jax.shard_map(
        on_device,
        mesh=mesh,
        in_specs=(P("ctx", None, None, "ch"), P(), P(), P(), P("ch"), P("ctx", "ch")),
        out_specs=(P("ctx", "ch"), P("ctx", None, "ch"), P(), P("ch")),
        check_vma=False,
    )
```

```python
import functools
import math

import jax
import jax.numpy as jnp
from jax import lax
from jax.experimental import pallas as pl
from jax.experimental.pallas import tpu as pltpu
from jax.sharding import PartitionSpec as P

BF16 = jnp.bfloat16
F32 = jnp.float32
SMEM = pltpu.SMEM
VMEM = pltpu.VMEM

BLK = 256
HOPS = 8
SLOTS = 6
ROWS = 4
LANES = 128
WIDE = 256
GROUP = 32
TAP_ROWS = 17
VLIM = 56 * 1024 * 1024


def hbm():
    return pl.BlockSpec(memory_space=pltpu.HBM)


def smem():
    return pl.BlockSpec(memory_space=SMEM)


def vmem():
    return pl.BlockSpec(memory_space=VMEM)


def choose_kernel(
    cycle, me_ref, target_ref, own_ref, up_ref, down_ref, code_ref, slot_ref, rows, sems
):
    me = me_ref[0]
    below = lax.rem(me + cycle - 1, cycle)
    above = lax.rem(me + 1, cycle)
    up_slot = jnp.int32(0)
    down_slot = jnp.int32(0)
    for k in range(SLOTS):
        shard = target_ref[0, me * SLOTS + k]
        up_slot = jnp.where(shard == above, k, up_slot)
        down_slot = jnp.where(shard == below, k, down_slot)
    copies = [
        pltpu.make_async_copy(own_ref.at[slot, n], rows.at[side, n], sems.at[side, n])
        for side, slot in enumerate((up_slot, down_slot))
        for n in range(3)
    ]
    for copy in copies:
        copy.start()
    for o in range(ROWS):
        code_ref[o] = 0
        slot_ref[o] = 0
    slot_ref[ROWS] = up_slot
    slot_ref[ROWS + 1] = down_slot
    for k in range(SLOTS):
        shard = target_ref[0, me * SLOTS + k]
        offset = target_ref[1, me * SLOTS + k]

        @pl.when(shard == me)
        def _():
            slot_ref[offset] = k

        for owner, code in ((below, 1), (above, 2)):
            their_shard = target_ref[0, owner * SLOTS + k]
            their_offset = target_ref[1, owner * SLOTS + k]

            @pl.when(their_shard == me)
            def _():
                code_ref[their_offset] = code

    for copy in copies:
        copy.wait()
    for side, to_ref in enumerate((up_ref, down_ref)):
        to_ref[0] = rows[side, 0]
        for n in range(rows.shape[-1] // WIDE):
            lanes = slice(n * WIDE, (n + 1) * WIDE)
            to_ref[1, :, lanes] = round_mul(rows[side, 1, :, lanes], rows[side, 2, :, lanes])


def later_kernel(slot_ref, own_ref, up_ref, down_ref, sems):
    copies = [
        pltpu.make_async_copy(own_ref.at[slot_ref[ROWS + n], pl.ds(1, 2)], to_ref, sems.at[n])
        for n, to_ref in enumerate((up_ref, down_ref))
    ]
    for copy in copies:
        copy.start()
    for copy in copies:
        copy.wait()


def tables_kernel(docs, length_ref, table_ref, count_ref):
    def one_doc(d, start):
        end = start + length_ref[d]
        table_ref[3, d] = start
        table_ref[4, d] = end

        def heads(b, carry):
            table_ref[0, b] = b - lax.shift_right_logical(start, 8)
            table_ref[1, b] = jnp.minimum(end - BLK * b, BLK)
            return carry

        def tails(b, carry):
            table_ref[2, b] = jnp.maximum(start - BLK * b, 0)
            table_ref[8, b] = lax.shift_right_logical(end - 1, 8) - b
            return carry

        lax.fori_loop(
            lax.shift_right_logical(start + BLK - 1, 8),
            lax.shift_right_logical(end + BLK - 1, 8),
            heads,
            0,
        )
        lax.fori_loop(
            lax.shift_right_logical(start, 8), lax.shift_right_logical(end, 8), tails, 0
        )
        return end

    lax.fori_loop(0, docs, one_doc, jnp.int32(0))

    for kind, (reach_row, order_row) in enumerate(((0, 5), (8, 9))):
        for n in range(HOPS + 1):
            count_ref[kind, n] = 0

        def count(b, carry):
            reach = table_ref[reach_row, b]
            count_ref[kind, reach] = count_ref[kind, reach] + 1
            return carry

        lax.fori_loop(0, docs, count, 0)
        before = jnp.int32(0)
        for n in range(HOPS, -1, -1):
            these = count_ref[kind, n]
            count_ref[kind, n] = before
            before = before + these

        def place(b, carry):
            reach = table_ref[reach_row, b]
            at = count_ref[kind, reach]
            count_ref[kind, reach] = at + 1
            table_ref[order_row, at] = b
            table_ref[order_row + 1, b] = at
            table_ref[order_row + 2, at] = reach
            return carry

        lax.fori_loop(0, docs, place, 0)


def make_bands(taps_ref, fwd_ref, bwd_ref):
    width = BLK * (HOPS + 2)
    part = 32
    for r in range(BLK // part):
        rows = jnp.broadcast_to(taps_ref[...], (part, width))
        rows = pltpu.roll(rows, part * r, 1, stride=1, stride_axis=0)
        for delta in range(HOPS + 1):
            at = BLK * (HOPS - delta) + part * r
            fwd_ref[at : at + part, :] = rows[:, BLK * (delta + 1) : BLK * (delta + 2)].astype(BF16)
    for delta in range(HOPS + 1):
        at = BLK * (HOPS - delta)
        bwd_ref[BLK * delta : BLK * (delta + 1), :] = fwd_ref[at : at + BLK, :].T


def round_mul(a, b):
    return (a.astype(F32) * b.astype(F32)).astype(BF16)


def write_row(sent_ref, lane, toks, read_product, read_grad_mid):
    peers, _, chans, _ = sent_ref.shape
    together = WIDE // chans
    for n in range(peers // together):
        lanes = slice(n * WIDE, (n + 1) * WIDE)
        to = slice(n * together, (n + 1) * together)
        for side, read in enumerate((read_product, read_grad_mid)):
            sent_ref[to, side, :, lane : lane + toks] = read(lanes).T.reshape(together, chans, toks)


def own_kernel(code_ref, slot_ref, own_ref, grad_ref, sent_ref, row, grad, sems):
    toks = row.shape[2]

    def copies(o):
        return (
            pltpu.make_async_copy(own_ref.at[slot_ref[o]], row.at[o], sems.at[o]),
            pltpu.make_async_copy(
                grad_ref.at[pl.ds(o * toks, toks)], grad.at[o], sems.at[ROWS + o]
            ),
        )

    for o in range(ROWS):
        for copy in copies(o):
            copy.start()
    for o in range(ROWS):
        for copy in copies(o):
            copy.wait()

        @pl.when(code_ref[o] == 0)
        def _():
            write_row(
                sent_ref,
                o * toks,
                toks,
                lambda c: round_mul(row[o, 1, :, c], row[o, 2, :, c]),
                lambda c: round_mul(grad[o, :, c], row[o, 0, :, c]),
            )


def guest_kernel(
    code_ref, low_ref, high_ref, grad_ref, part_ref, sent_ref, guest, grad, ready, in_sems, out_sems
):
    del part_ref
    _, peers, _, chans, toks = ready.shape
    together = WIDE // chans
    parts = peers // together
    guests = []
    for n, ref in enumerate((low_ref, high_ref)):
        at = jnp.int32(0)
        for o in range(ROWS):
            at = jnp.where(code_ref[o] == n + 1, o + 1, at)
        here = pl.ds(pl.multiple_of(jnp.maximum(at - 1, 0) * toks, toks), toks)
        into = [
            pltpu.make_async_copy(ref, guest.at[n], in_sems.at[n, 0]),
            pltpu.make_async_copy(grad_ref.at[here], grad.at[n], in_sems.at[n, 1]),
        ]
        out = []
        for m in range(parts):
            to = pl.ds(m * together, together)
            out.append(
                pltpu.make_async_copy(
                    ready.at[n, to], sent_ref.at[to, :, :, here], out_sems.at[n, m]
                )
            )
        guests.append((n, at > 0, into, out))
    for n, live, into, out in guests:

        @pl.when(live)
        def _():
            for copy in into:
                copy.start()

    for n, live, into, out in guests:

        @pl.when(live)
        def _():
            for copy in into:
                copy.wait()
            for m in range(parts):
                lanes = slice(m * WIDE, (m + 1) * WIDE)
                to = slice(m * together, (m + 1) * together)
                grad_mid = round_mul(grad[n, :, lanes], guest[n, 0, :, lanes])
                ready[n, to, 0] = guest[n, 1, :, lanes].T.reshape(together, chans, toks)
                ready[n, to, 1] = grad_mid.T.reshape(together, chans, toks)
                out[m].start()

    for n, live, into, out in guests:

        @pl.when(live)
        def _():
            for copy in out:
                copy.wait()


def place_of(b, peers):
    src = jnp.where(b < peers, b, 2 * peers - 1 - b)
    lane = pl.multiple_of(jnp.where(b < peers, 0, BLK), BLK)
    return src, lane


def dot(a, b):
    return jnp.dot(a, b, preferred_element_type=F32)


def long_kernel(
    me_ref, table_ref, got_ref, taps_ref, out_ref,
    fwd_ref, bwd_ref, x_all, z_all, x_tail, z_head, z_back, xd, zd, ze, turned, doc_near, doc_back,
    near, far_sum, back_near, back_far, pairs, extra,
):
    peers = got_ref.shape[0]
    ch = got_ref.shape[2]
    blocks = 2 * peers
    docs = blocks
    rows = blocks * ch
    pad = HOPS * ch
    far = HOPS * BLK
    lane = lax.broadcasted_iota(jnp.int32, (ch, BLK), 1)

    make_bands(taps_ref, fwd_ref, bwd_ref)
    x_tail[0:pad, :] = jnp.zeros((pad, BLK), BF16)
    z_head[rows : rows + pad, :] = jnp.zeros((pad, BLK), BF16)
    back_far[...] = jnp.zeros_like(back_far)
    far_sum[...] = jnp.zeros_like(far_sum)
    pairs[...] = jnp.zeros_like(pairs)

    def spread(k, total):
        b = table_ref[5, k]
        src, at_lane = place_of(b, peers)
        at = pl.multiple_of(b * ch, ch)
        x = got_ref[src, 0, :, pl.ds(at_lane, BLK)]
        z = got_ref[src, 1, :, pl.ds(at_lane, BLK)]
        x_all[pl.ds(at, ch), :] = x
        z_all[pl.ds(at, ch), :] = z
        end, tail = table_ref[1, b], table_ref[2, b]
        x_f, z_f = x.astype(F32), z.astype(F32)
        x_tail[pl.ds(at + pad, ch), :] = jnp.where(lane >= tail, x_f, 0).astype(BF16)
        z_cut = jnp.where(lane < end, z_f, 0).astype(BF16)
        z_head[pl.ds(at, ch), :] = z_cut
        z_back[pl.ds(pl.multiple_of(k * ch, ch), ch), :] = z_cut
        return total + x_f * z_f

    skip = lax.fori_loop(0, blocks, spread, jnp.zeros((ch, BLK), F32), unroll=4)

    def doc_parts(d):
        start, end = table_ref[3, d], table_ref[4, d]
        end_block = lax.shift_right_logical(end - 1, 8)
        end_at = jnp.bitwise_and(end, BLK - 1)
        end_from = jnp.maximum(start - BLK * end_block, 0)
        start_block = lax.shift_right_logical(start, 8)
        start_at = jnp.bitwise_and(start, BLK - 1)
        start_at = jnp.where(start_at == 0, BLK, start_at)
        start_to = end - BLK * start_block
        return end_block, end_from, end_at, start_block, start_at, start_to

    def spread_docs(d, carry):
        end_block, end_from, end_at, start_block, start_at, start_to = doc_parts(d)
        at = pl.multiple_of(d * ch, ch)
        at_end = pl.multiple_of(end_block * ch, ch)
        at_start = pl.multiple_of(start_block * ch, ch)
        ends = (lane >= end_from) & (lane < end_at)
        begins = (lane >= start_at) & (lane < start_to)
        x = x_all[pl.ds(at_end, ch), :].astype(F32)
        z = z_all[pl.ds(at_end, ch), :].astype(F32)
        z2 = z_all[pl.ds(at_start, ch), :].astype(F32)
        xd[pl.ds(at, ch), :] = jnp.where(ends, x, 0).astype(BF16)
        zd[pl.ds(at, ch), :] = jnp.where(ends, z, 0).astype(BF16)
        ze[pl.ds(at, ch), :] = jnp.where(begins, z2, 0).astype(BF16)
        return carry

    lax.fori_loop(0, docs, spread_docs, 0, unroll=4)

    step = 256
    first_fwd = fwd_ref.at[far : far + BLK, :]
    first_bwd = bwd_ref.at[0:BLK, :]

    def inner(c, carry):
        at = pl.multiple_of(c * step, step)
        here = pl.ds(at, step)
        z = z_head[here, :]
        x = jnp.concatenate([x_tail[pl.ds(at + pad, step), :], xd[here, :]], axis=0)
        ahead = dot(x, first_fwd[...])
        near[here, :] = ahead[:step]
        doc_near[here, :] = ahead[step:]
        behind = dot(jnp.concatenate([z, ze[here, :]], axis=0), first_bwd[...])
        back_near[here, :] = behind[:step]
        doc_back[here, :] = behind[step:]
        turned[:, here] = z_back[here, :].T
        pairs[:, far:] += dot(jnp.concatenate([z_all[here, :].T, zd[here, :].T], axis=1), x)
        return carry

    lax.fori_loop(0, rows // step, inner, 0)

    def add_docs(d, carry):
        end_block, end_from, end_at, start_block, start_at, start_to = doc_parts(d)
        here = pl.ds(pl.multiple_of(d * ch, ch), ch)
        at_end = pl.multiple_of(end_block * ch, ch)
        at_start = pl.multiple_of(start_block * ch, ch)
        near[pl.ds(at_end, ch), :] += jnp.where(lane < end_at, doc_near[here, :], 0.0)
        back_near[pl.ds(at_start, ch), :] += jnp.where(lane >= start_at, doc_back[here, :], 0.0)
        return carry

    lax.fori_loop(0, docs, add_docs, 0, unroll=4)

    wide = GROUP * ch

    def collect(c, order_row, source, by, delta, empty):
        tiles = []
        for i in range(GROUP):
            k = c * GROUP + i
            inside = table_ref[order_row + 2, k] >= delta
            at = jnp.where(inside, table_ref[order_row, k] + by, empty)
            tiles.append(source[pl.ds(pl.multiple_of(at * ch, ch), ch), :])
        return jnp.concatenate(tiles, axis=0)

    def outer(c, carry):
        here = pl.ds(pl.multiple_of(c * wide, wide), wide)
        reach_back, reach_ahead = table_ref[7, c * GROUP], table_ref[11, c * GROUP]
        for reach in range(1, HOPS + 1):

            @pl.when(reach_back == reach)
            def _():
                x = jnp.concatenate(
                    [collect(c, 5, x_tail, HOPS - n, n, 0) for n in range(reach, 0, -1)], axis=1
                )
                lags = slice((HOPS - reach) * BLK, far)
                far_sum[here, :] = dot(x, fwd_ref[lags, :])
                pairs[:, lags] += dot(turned[:, here], x)

            @pl.when(reach_ahead == reach)
            def _():
                z = jnp.concatenate(
                    [collect(c, 9, z_head, n, n, blocks) for n in range(1, reach + 1)], axis=1
                )
                back_far[here, :] = dot(z, bwd_ref[BLK : (reach + 1) * BLK, :])

        return carry

    lax.fori_loop(0, blocks // GROUP, outer, 0)

    def gather_out(k, carry):
        b = table_ref[5, k]
        src, at_lane = place_of(b, peers)
        here = pl.ds(pl.multiple_of(k * ch, ch), ch)
        at = pl.multiple_of(b * ch, ch)
        ahead = jnp.where(lane < table_ref[1, b], far_sum[here, :], 0.0)
        ahead_at = pl.multiple_of(table_ref[10, b] * ch, ch)
        behind = jnp.where(lane >= table_ref[2, b], back_far[pl.ds(ahead_at, ch), :], 0.0)
        out_ref[src, 0, :, pl.ds(at_lane, BLK)] = (near[pl.ds(at, ch), :] + ahead).astype(BF16)
        out_ref[src, 1, :, pl.ds(at_lane, BLK)] = (back_near[pl.ds(at, ch), :] + behind).astype(BF16)
        return carry

    lax.fori_loop(0, blocks, gather_out, 0, unroll=4)

    total = jnp.zeros((8, far + 2 * BLK), F32)
    for r in range(BLK // 8):
        band = jnp.concatenate([pairs[8 * r : 8 * (r + 1), :], jnp.zeros((8, BLK), F32)], axis=1)
        total = total + pltpu.roll(band, BLK - 8 - 8 * r, 1)
    lags = total[7:8]
    for r in range(7):
        lags = lags + pltpu.roll(total[r : r + 1], 7 - r, 1)
    extra[...] = jnp.zeros_like(extra)
    count = TAP_ROWS
    for r in range(count):
        at = far + BLK - LANES * (r + 1)
        extra[r : r + 1, :] = lags[:, at : at + LANES]
    r_id = lax.broadcasted_iota(jnp.int32, (LANES, LANES), 0)
    c_id = lax.broadcasted_iota(jnp.int32, (LANES, LANES), 1)
    anti = jnp.where(r_id + c_id == LANES - 1, 1.0, 0.0).astype(BF16)
    extra[...] = dot(extra[...].astype(BF16), anti)

    by_channel = jnp.sum(skip, axis=1, keepdims=True)
    e_row = lax.broadcasted_iota(jnp.int32, (ch, LANES), 0)
    e_col = lax.broadcasted_iota(jnp.int32, (ch, LANES), 1)
    mine = e_row + ch * lax.rem(me_ref[0], LANES // ch) == e_col
    skip_row = jnp.sum(jnp.where(mine, by_channel, 0.0), axis=0, keepdims=True)
    high = skip_row.astype(BF16).astype(F32)
    extra[count : count + 1, :] = high
    extra[count + 1 : count + 2, :] = skip_row - high
    packed = extra[...].astype(BF16)
    for side in range(2):
        out_ref[:, side, :, 2 * BLK : 2 * BLK + LANES] = jnp.broadcast_to(
            packed[side * ch : (side + 1) * ch][None], (peers, ch, LANES)
        )


def finish_kernel(
    code_ref, slot_ref, gain_ref, own_ref, low_ref, high_ref, grad_ref,
    low_kv_ref, high_kv_ref, got_ref, y_ref, grads_ref,
    row, grad, got, y_row, grads_row, in_sems, out_sems,
):
    _, peers, _, chans, toks = got.shape

    def here(o):
        return pl.ds(o * toks, toks)

    def fetch(o, act):
        code = code_ref[o]

        @pl.when(code == 0)
        def _():
            act(pltpu.make_async_copy(own_ref.at[slot_ref[o]], row.at[o], in_sems.at[o, 0]))

        for n, first, later in ((1, low_ref, low_kv_ref), (2, high_ref, high_kv_ref)):

            @pl.when(code == n)
            def _():
                act(pltpu.make_async_copy(first.at[0], row.at[o, 0], in_sems.at[o, 0]))
                act(pltpu.make_async_copy(later, row.at[o, pl.ds(1, 2)], in_sems.at[o, 1]))

        act(pltpu.make_async_copy(grad_ref.at[here(o)], grad.at[o], in_sems.at[o, 2]))
        act(pltpu.make_async_copy(got_ref.at[:, :, :, here(o)], got.at[o], in_sems.at[o, 3]))

    def results(o, act):
        act(pltpu.make_async_copy(y_row.at[o], y_ref.at[here(o)], out_sems.at[o, 0]))
        for n in range(3):
            act(
                pltpu.make_async_copy(
                    grads_row.at[o, n], grads_ref.at[n, here(o)], out_sems.at[o, 1 + n]
                )
            )

    together = WIDE // chans
    for o in range(ROWS):
        fetch(o, lambda copy: copy.start())
    for o in range(ROWS):
        fetch(o, lambda copy: copy.wait())
        for n in range(peers // together):
            lanes = slice(n * WIDE, (n + 1) * WIDE)
            of = slice(n * together, (n + 1) * together)
            conv = got[o, of, 0].reshape(WIDE, toks).T.astype(F32)
            back = got[o, of, 1].reshape(WIDE, toks).T.astype(F32)
            query, key_in, value = (row[o, s, :, lanes].astype(F32) for s in range(3))
            out_grad = grad[o, :, lanes].astype(F32)
            gain = gain_ref[:, lanes]
            product = (key_in * value).astype(BF16).astype(F32)
            grad_mid = (out_grad * query).astype(BF16).astype(F32)
            mixed = conv + gain * product
            grad_x = back + gain * grad_mid
            y_row[o, :, lanes] = (query * mixed).astype(BF16)
            grads_row[o, 0, :, lanes] = (out_grad * mixed).astype(BF16)
            grads_row[o, 1, :, lanes] = (grad_x * value).astype(BF16)
            grads_row[o, 2, :, lanes] = (grad_x * key_in).astype(BF16)
        results(o, lambda copy: copy.start())
    for o in range(ROWS):
        results(o, lambda copy: copy.wait())


def totals_kernel(tap_scale, skip_scale, part_ref, taps_ref, skip_ref):
    filters = taps_ref.shape[0]
    peers, _, ch, lanes = part_ref.shape
    group = peers // filters
    for f in range(filters):
        part = part_ref[f * group : (f + 1) * group].astype(F32)
        total = jnp.sum(part, axis=0) * tap_scale
        for r in range(TAP_ROWS):
            row = total[r // ch, r % ch : r % ch + 1]
            taps_ref[f : f + 1, r * lanes : (r + 1) * lanes] = row
    at = TAP_ROWS - ch
    together = lanes // ch
    for r in range(peers // together):
        part = part_ref[r * together : (r + 1) * together, 1, :, :].astype(F32)
        total = jnp.sum(part, axis=0) * skip_scale
        skip_ref[r : r + 1, :] = total[at : at + 1] + total[at + 1 : at + 2]


def shifted(array, axis, by):
    length = lax.axis_size(axis)
    return lax.ppermute(array, axis, [(i, (i + by) % length) for i in range(length)])


def on_device(rollout_rows, pack_targets, doc_lengths, filter_taps, skip_gain, out_grad):
    peers = lax.axis_size("ctx")
    index = lax.axis_index("ctx").astype(jnp.int32)
    slots, row_len, streams, channels = rollout_rows.shape
    tokens = out_grad.shape[0]
    filters, tap_count = filter_taps.shape
    docs = doc_lengths.shape[0]
    ch = channels // peers
    blocks = 2 * peers
    own = rollout_rows.transpose(0, 2, 1, 3)
    half_shape = jax.ShapeDtypeStruct((2, row_len, channels), BF16)
    up, down, code, slot = pl.pallas_call(
        functools.partial(choose_kernel, peers),
        out_shape=(
            half_shape,
            half_shape,
            jax.ShapeDtypeStruct((ROWS,), jnp.int32),
            jax.ShapeDtypeStruct((ROWS + 2,), jnp.int32),
        ),
        in_specs=[smem(), smem(), hbm()],
        out_specs=(vmem(), vmem(), smem(), smem()),
        scratch_shapes=[
            VMEM((2, streams, row_len, channels), BF16),
            pltpu.SemaphoreType.DMA((2, 3)),
        ],
        compiler_params=pltpu.CompilerParams(vmem_limit_bytes=VLIM),
        name="choose",
    )(index[None], pack_targets.T, own)
    up_kv, down_kv = pl.pallas_call(
        later_kernel,
        out_shape=(half_shape, half_shape),
        in_specs=[smem(), hbm()],
        out_specs=(vmem(), vmem()),
        scratch_shapes=[pltpu.SemaphoreType.DMA((2,))],
        compiler_params=pltpu.CompilerParams(vmem_limit_bytes=VLIM),
        cost_estimate=pl.CostEstimate(flops=0, bytes_accessed=6_000_000, transcendentals=0),
        name="later",
    )(slot, own)
    low = shifted(up, "ctx", 1)
    high = shifted(down, "ctx", -1)

    mine = lax.dynamic_index_in_dim(filter_taps, index // (peers // filters), 0, keepdims=True)
    mine = mine.astype(BF16).astype(F32)
    mine = jnp.pad(mine, [(0, 0), (BLK, BLK * (HOPS + 1) - tap_count)])
    table = pl.pallas_call(
        functools.partial(tables_kernel, docs),
        out_shape=jax.ShapeDtypeStruct((16, docs), jnp.int32),
        in_specs=[smem()],
        out_specs=smem(),
        scratch_shapes=[SMEM((2, HOPS + 1), jnp.int32)],
        compiler_params=pltpu.CompilerParams(vmem_limit_bytes=4 * 1024 * 1024),
        cost_estimate=pl.CostEstimate(flops=0, bytes_accessed=20_000_000, transcendentals=0),
        name="tables",
    )(doc_lengths)

    sent_shape = jax.ShapeDtypeStruct((peers, 2, ch, tokens), BF16)
    row_buffers = [
        VMEM((ROWS, streams, row_len, channels), BF16),
        VMEM((ROWS, row_len, channels), BF16),
    ]
    part = pl.pallas_call(
        own_kernel,
        out_shape=sent_shape,
        in_specs=[smem(), smem(), hbm(), hbm()],
        out_specs=vmem(),
        scratch_shapes=row_buffers + [pltpu.SemaphoreType.DMA((2 * ROWS,))],
        compiler_params=pltpu.CompilerParams(vmem_limit_bytes=VLIM),
        cost_estimate=pl.CostEstimate(flops=0, bytes_accessed=20_000_000, transcendentals=0),
        name="own_products",
    )(code, slot, own, out_grad)
    sent = pl.pallas_call(
        guest_kernel,
        out_shape=sent_shape,
        in_specs=[smem(), hbm(), hbm(), hbm(), hbm()],
        out_specs=hbm(),
        scratch_shapes=[
            VMEM((2, 2, row_len, channels), BF16),
            VMEM((2, row_len, channels), BF16),
            VMEM((2, peers, 2, ch, row_len), BF16),
            pltpu.SemaphoreType.DMA((2, 2)),
            pltpu.SemaphoreType.DMA((2, channels // WIDE)),
        ],
        input_output_aliases={4: 0},
        compiler_params=pltpu.CompilerParams(vmem_limit_bytes=VLIM),
        name="guest_products",
    )(code, low, high, out_grad, part)
    got = lax.all_to_all(sent, "ctx", 0, 0, tiled=True)
    up_kv, down_kv, got = lax.optimization_barrier((up_kv, down_kv, got))
    low_kv = shifted(up_kv, "ctx", 1)
    high_kv = shifted(down_kv, "ctx", -1)

    rows = blocks * ch
    pad = HOPS * ch
    reply = pl.pallas_call(
        long_kernel,
        out_shape=jax.ShapeDtypeStruct((peers, 2, ch, tokens + LANES), BF16),
        in_specs=[smem(), smem(), vmem(), vmem()],
        out_specs=vmem(),
        scratch_shapes=[
            VMEM((BLK * (HOPS + 1), BLK), BF16),
            VMEM((BLK * (HOPS + 1), BLK), BF16),
            VMEM((rows, BLK), BF16),
            VMEM((rows, BLK), BF16),
            VMEM((rows + pad, BLK), BF16),
            VMEM((rows + pad, BLK), BF16),
            VMEM((rows, BLK), BF16),
            VMEM((rows, BLK), BF16),
            VMEM((rows, BLK), BF16),
            VMEM((rows, BLK), BF16),
            VMEM((BLK, rows), BF16),
            VMEM((rows, BLK), F32),
            VMEM((rows, BLK), F32),
            VMEM((rows, BLK), F32),
            VMEM((rows, BLK), F32),
            VMEM((rows, BLK), F32),
            VMEM((rows, BLK), F32),
            VMEM((BLK, BLK * (HOPS + 1)), F32),
            VMEM((2 * ch, LANES), F32),
        ],
        compiler_params=pltpu.CompilerParams(vmem_limit_bytes=34 * 1024 * 1024),
        cost_estimate=pl.CostEstimate(
            flops=2 * 30 * rows * BLK * BLK, bytes_accessed=7_000_000, transcendentals=0
        ),
        name="long_filter",
    )(index[None], table, got, mine)
    low_kv, high_kv, reply = lax.optimization_barrier((low_kv, high_kv, reply))
    back = lax.all_to_all(reply, "ctx", 0, 0, tiled=True)

    seq_total = tokens * peers
    chan_total = channels * lax.axis_size("ch")
    tap_sum, skip_sum = pl.pallas_call(
        functools.partial(
            totals_kernel,
            1.0 / math.sqrt(seq_total * chan_total / filters),
            1.0 / math.sqrt(seq_total),
        ),
        out_shape=(
            jax.ShapeDtypeStruct((filters, TAP_ROWS * LANES), F32),
            jax.ShapeDtypeStruct((channels // LANES, LANES), F32),
        ),
        grid=(1,),
        in_specs=[
            pl.BlockSpec((peers, 2, ch, LANES), lambda o: (0, 0, 0, tokens // LANES)),
        ],
        out_specs=(
            pl.BlockSpec((filters, TAP_ROWS * LANES), lambda o: (0, 0)),
            pl.BlockSpec((channels // LANES, LANES), lambda o: (0, 0)),
        ),
        name="totals",
    )(back)
    other = lax.ppermute(tap_sum, "ch", [(0, 1), (1, 0)])

    out_y, grads = pl.pallas_call(
        finish_kernel,
        out_shape=(
            jax.ShapeDtypeStruct((tokens, channels), BF16),
            jax.ShapeDtypeStruct((streams, tokens, channels), BF16),
        ),
        in_specs=[smem(), smem(), vmem()] + [hbm()] * 7,
        out_specs=(hbm(), hbm()),
        scratch_shapes=row_buffers
        + [
            VMEM((ROWS, peers, 2, ch, row_len), BF16),
            VMEM((ROWS, row_len, channels), BF16),
            VMEM((ROWS, streams, row_len, channels), BF16),
            pltpu.SemaphoreType.DMA((ROWS, 4)),
            pltpu.SemaphoreType.DMA((ROWS, 4)),
        ],
        compiler_params=pltpu.CompilerParams(vmem_limit_bytes=VLIM),
        name="finish",
    )(code, slot, skip_gain[None], own, low, high, out_grad, low_kv, high_kv, back)

    grad_taps = (tap_sum + other)[:, :tap_count]
    grad_skip = skip_sum.reshape(channels)
    return (out_y, grads.transpose(1, 0, 2), grad_taps, grad_skip)


def solution(mesh):
    return jax.shard_map(
        on_device,
        mesh=mesh,
        in_specs=(P("ctx", None, None, "ch"), P(), P(), P(), P("ch"), P("ctx", "ch")),
        out_specs=(P("ctx", "ch"), P("ctx", None, "ch"), P(), P("ch")),
        check_vma=False,
    )
```

```python
import functools
import math

import jax
import jax.numpy as jnp
from jax import lax
from jax.experimental import pallas as pl
from jax.experimental.pallas import tpu as pltpu
from jax.sharding import PartitionSpec as P

BF16 = jnp.bfloat16
F32 = jnp.float32
SMEM = pltpu.SMEM
VMEM = pltpu.VMEM

BLK = 256
HOPS = 8
SLOTS = 6
ROWS = 4
LANES = 128
WIDE = 256
GROUP = 32
TAP_ROWS = 17
VLIM = 56 * 1024 * 1024


def hbm():
    return pl.BlockSpec(memory_space=pltpu.HBM)


def smem():
    return pl.BlockSpec(memory_space=SMEM)


def vmem():
    return pl.BlockSpec(memory_space=VMEM)


def choose_kernel(
    cycle, me_ref, target_ref, own_ref, up_ref, down_ref, code_ref, slot_ref, rows, sems
):
    me = me_ref[0]
    below = lax.rem(me + cycle - 1, cycle)
    above = lax.rem(me + 1, cycle)
    up_slot = jnp.int32(0)
    down_slot = jnp.int32(0)
    for k in range(SLOTS):
        shard = target_ref[0, me * SLOTS + k]
        up_slot = jnp.where(shard == above, k, up_slot)
        down_slot = jnp.where(shard == below, k, down_slot)
    copies = [
        pltpu.make_async_copy(own_ref.at[slot, n], rows.at[side, n], sems.at[side, n])
        for side, slot in enumerate((up_slot, down_slot))
        for n in range(3)
    ]
    for copy in copies:
        copy.start()
    for o in range(ROWS):
        code_ref[o] = 0
        slot_ref[o] = 0
    slot_ref[ROWS] = up_slot
    slot_ref[ROWS + 1] = down_slot
    for k in range(SLOTS):
        shard = target_ref[0, me * SLOTS + k]
        offset = target_ref[1, me * SLOTS + k]

        @pl.when(shard == me)
        def _():
            slot_ref[offset] = k

        for owner, code in ((below, 1), (above, 2)):
            their_shard = target_ref[0, owner * SLOTS + k]
            their_offset = target_ref[1, owner * SLOTS + k]

            @pl.when(their_shard == me)
            def _():
                code_ref[their_offset] = code

    for copy in copies:
        copy.wait()
    for side, to_ref in enumerate((up_ref, down_ref)):
        to_ref[0] = rows[side, 0]
        for n in range(rows.shape[-1] // WIDE):
            lanes = slice(n * WIDE, (n + 1) * WIDE)
            to_ref[1, :, lanes] = round_mul(rows[side, 1, :, lanes], rows[side, 2, :, lanes])


def later_kernel(slot_ref, own_ref, up_ref, down_ref, sems):
    copies = [
        pltpu.make_async_copy(own_ref.at[slot_ref[ROWS + n], pl.ds(1, 2)], to_ref, sems.at[n])
        for n, to_ref in enumerate((up_ref, down_ref))
    ]
    for copy in copies:
        copy.start()
    for copy in copies:
        copy.wait()


def tables_kernel(docs, length_ref, table_ref, count_ref):
    def one_doc(d, start):
        end = start + length_ref[d]
        table_ref[3, d] = start
        table_ref[4, d] = end

        def heads(b, carry):
            table_ref[0, b] = b - lax.shift_right_logical(start, 8)
            table_ref[1, b] = jnp.minimum(end - BLK * b, BLK)
            return carry

        def tails(b, carry):
            table_ref[2, b] = jnp.maximum(start - BLK * b, 0)
            table_ref[8, b] = lax.shift_right_logical(end - 1, 8) - b
            return carry

        lax.fori_loop(
            lax.shift_right_logical(start + BLK - 1, 8),
            lax.shift_right_logical(end + BLK - 1, 8),
            heads,
            0,
        )
        lax.fori_loop(
            lax.shift_right_logical(start, 8), lax.shift_right_logical(end, 8), tails, 0
        )
        return end

    lax.fori_loop(0, docs, one_doc, jnp.int32(0))

    for kind, (reach_row, order_row) in enumerate(((0, 5), (8, 9))):
        for n in range(HOPS + 1):
            count_ref[kind, n] = 0

        def count(b, carry):
            reach = table_ref[reach_row, b]
            count_ref[kind, reach] = count_ref[kind, reach] + 1
            return carry

        lax.fori_loop(0, docs, count, 0)
        before = jnp.int32(0)
        for n in range(HOPS, -1, -1):
            these = count_ref[kind, n]
            count_ref[kind, n] = before
            before = before + these

        def place(b, carry):
            reach = table_ref[reach_row, b]
            at = count_ref[kind, reach]
            count_ref[kind, reach] = at + 1
            table_ref[order_row, at] = b
            table_ref[order_row + 1, b] = at
            table_ref[order_row + 2, at] = reach
            return carry

        lax.fori_loop(0, docs, place, 0)


def make_bands(taps_ref, fwd_ref, bwd_ref):
    width = BLK * (HOPS + 2)
    part = 32
    for r in range(BLK // part):
        rows = jnp.broadcast_to(taps_ref[...], (part, width))
        rows = pltpu.roll(rows, part * r, 1, stride=1, stride_axis=0)
        for delta in range(HOPS + 1):
            at = BLK * (HOPS - delta) + part * r
            fwd_ref[at : at + part, :] = rows[:, BLK * (delta + 1) : BLK * (delta + 2)].astype(BF16)
    for delta in range(HOPS + 1):
        at = BLK * (HOPS - delta)
        bwd_ref[BLK * delta : BLK * (delta + 1), :] = fwd_ref[at : at + BLK, :].T


def round_mul(a, b):
    return (a.astype(F32) * b.astype(F32)).astype(BF16)


def write_row(sent_ref, lane, toks, read_product, read_grad_mid):
    peers, _, chans, _ = sent_ref.shape
    together = WIDE // chans
    for n in range(peers // together):
        lanes = slice(n * WIDE, (n + 1) * WIDE)
        to = slice(n * together, (n + 1) * together)
        for side, read in enumerate((read_product, read_grad_mid)):
            sent_ref[to, side, :, lane : lane + toks] = read(lanes).T.reshape(together, chans, toks)


def own_kernel(code_ref, slot_ref, own_ref, grad_ref, sent_ref, row, grad, sems):
    toks = row.shape[2]

    def copies(o):
        return (
            pltpu.make_async_copy(own_ref.at[slot_ref[o]], row.at[o], sems.at[o]),
            pltpu.make_async_copy(
                grad_ref.at[pl.ds(o * toks, toks)], grad.at[o], sems.at[ROWS + o]
            ),
        )

    for o in range(ROWS):
        for copy in copies(o):
            copy.start()
    for o in range(ROWS):
        for copy in copies(o):
            copy.wait()

        @pl.when(code_ref[o] == 0)
        def _():
            write_row(
                sent_ref,
                o * toks,
                toks,
                lambda c: round_mul(row[o, 1, :, c], row[o, 2, :, c]),
                lambda c: round_mul(grad[o, :, c], row[o, 0, :, c]),
            )


def guest_kernel(
    code_ref, low_ref, high_ref, grad_ref, part_ref, sent_ref, guest, grad, ready, in_sems, out_sems
):
    del part_ref
    _, peers, _, chans, toks = ready.shape
    together = WIDE // chans
    parts = peers // together
    guests = []
    for n, ref in enumerate((low_ref, high_ref)):
        at = jnp.int32(0)
        for o in range(ROWS):
            at = jnp.where(code_ref[o] == n + 1, o + 1, at)
        here = pl.ds(pl.multiple_of(jnp.maximum(at - 1, 0) * toks, toks), toks)
        into = [
            pltpu.make_async_copy(ref, guest.at[n], in_sems.at[n, 0]),
            pltpu.make_async_copy(grad_ref.at[here], grad.at[n], in_sems.at[n, 1]),
        ]
        out = []
        for m in range(parts):
            to = pl.ds(m * together, together)
            out.append(
                pltpu.make_async_copy(
                    ready.at[n, to], sent_ref.at[to, :, :, here], out_sems.at[n, m]
                )
            )
        guests.append((n, at > 0, into, out))
    for n, live, into, out in guests:

        @pl.when(live)
        def _():
            for copy in into:
                copy.start()

    for n, live, into, out in guests:

        @pl.when(live)
        def _():
            for copy in into:
                copy.wait()
            for m in range(parts):
                lanes = slice(m * WIDE, (m + 1) * WIDE)
                to = slice(m * together, (m + 1) * together)
                grad_mid = round_mul(grad[n, :, lanes], guest[n, 0, :, lanes])
                ready[n, to, 0] = guest[n, 1, :, lanes].T.reshape(together, chans, toks)
                ready[n, to, 1] = grad_mid.T.reshape(together, chans, toks)
                out[m].start()

    for n, live, into, out in guests:

        @pl.when(live)
        def _():
            for copy in out:
                copy.wait()


def place_of(b, peers):
    src = jnp.where(b < peers, b, 2 * peers - 1 - b)
    lane = pl.multiple_of(jnp.where(b < peers, 0, BLK), BLK)
    return src, lane


def dot(a, b):
    return jnp.dot(a, b, preferred_element_type=F32)


def long_kernel(
    me_ref, table_ref, got_ref, taps_ref, out_ref,
    fwd_ref, bwd_ref, x_all, z_all, x_tail, z_head, z_back, xd, zd, ze, turned, doc_near, doc_back,
    near, far_sum, back_near, back_far, pairs, extra,
):
    peers = got_ref.shape[0]
    ch = got_ref.shape[2]
    blocks = 2 * peers
    docs = blocks
    rows = blocks * ch
    pad = HOPS * ch
    far = HOPS * BLK
    lane = lax.broadcasted_iota(jnp.int32, (ch, BLK), 1)

    make_bands(taps_ref, fwd_ref, bwd_ref)
    x_tail[0:pad, :] = jnp.zeros((pad, BLK), BF16)
    z_head[rows : rows + pad, :] = jnp.zeros((pad, BLK), BF16)
    pairs[...] = jnp.zeros_like(pairs)

    def spread(k, total):
        b = table_ref[5, k]
        src, at_lane = place_of(b, peers)
        at = pl.multiple_of(b * ch, ch)
        x = got_ref[src, 0, :, pl.ds(at_lane, BLK)]
        z = got_ref[src, 1, :, pl.ds(at_lane, BLK)]
        x_all[pl.ds(at, ch), :] = x
        z_all[pl.ds(at, ch), :] = z
        end, tail = table_ref[1, b], table_ref[2, b]
        x_f, z_f = x.astype(F32), z.astype(F32)
        x_tail[pl.ds(at + pad, ch), :] = jnp.where(lane >= tail, x_f, 0).astype(BF16)
        z_cut = jnp.where(lane < end, z_f, 0).astype(BF16)
        z_head[pl.ds(at, ch), :] = z_cut
        z_back[pl.ds(pl.multiple_of(k * ch, ch), ch), :] = z_cut
        return total + x_f * z_f

    skip = lax.fori_loop(0, blocks, spread, jnp.zeros((ch, BLK), F32), unroll=4)

    def doc_parts(d):
        start, end = table_ref[3, d], table_ref[4, d]
        end_block = lax.shift_right_logical(end - 1, 8)
        end_at = jnp.bitwise_and(end, BLK - 1)
        end_from = jnp.maximum(start - BLK * end_block, 0)
        start_block = lax.shift_right_logical(start, 8)
        start_at = jnp.bitwise_and(start, BLK - 1)
        start_at = jnp.where(start_at == 0, BLK, start_at)
        start_to = end - BLK * start_block
        return end_block, end_from, end_at, start_block, start_at, start_to

    def spread_docs(d, carry):
        end_block, end_from, end_at, start_block, start_at, start_to = doc_parts(d)
        at = pl.multiple_of(d * ch, ch)
        at_end = pl.multiple_of(end_block * ch, ch)
        at_start = pl.multiple_of(start_block * ch, ch)
        ends = (lane >= end_from) & (lane < end_at)
        begins = (lane >= start_at) & (lane < start_to)
        x = x_all[pl.ds(at_end, ch), :].astype(F32)
        z = z_all[pl.ds(at_end, ch), :].astype(F32)
        z2 = z_all[pl.ds(at_start, ch), :].astype(F32)
        xd[pl.ds(at, ch), :] = jnp.where(ends, x, 0).astype(BF16)
        zd[pl.ds(at, ch), :] = jnp.where(ends, z, 0).astype(BF16)
        ze[pl.ds(at, ch), :] = jnp.where(begins, z2, 0).astype(BF16)
        return carry

    lax.fori_loop(0, docs, spread_docs, 0, unroll=4)

    step = 512
    first_fwd = fwd_ref.at[far : far + BLK, :]
    first_bwd = bwd_ref.at[0:BLK, :]

    def inner(c, carry):
        at = pl.multiple_of(c * step, step)
        here = pl.ds(at, step)
        z = z_head[here, :]
        x = jnp.concatenate([x_tail[pl.ds(at + pad, step), :], xd[here, :]], axis=0)
        ahead = dot(x, first_fwd[...])
        near[here, :] = ahead[:step]
        doc_near[here, :] = ahead[step:]
        behind = dot(jnp.concatenate([z, ze[here, :]], axis=0), first_bwd[...])
        back_near[here, :] = behind[:step]
        doc_back[here, :] = behind[step:]
        turned[:, here] = z_back[here, :].T
        pairs[:, far:] += dot(jnp.concatenate([z_all[here, :].T, zd[here, :].T], axis=1), x)
        return carry

    lax.fori_loop(0, rows // step, inner, 0)

    def add_docs(d, carry):
        end_block, end_from, end_at, start_block, start_at, start_to = doc_parts(d)
        here = pl.ds(pl.multiple_of(d * ch, ch), ch)
        at_end = pl.multiple_of(end_block * ch, ch)
        at_start = pl.multiple_of(start_block * ch, ch)
        near[pl.ds(at_end, ch), :] += jnp.where(lane < end_at, doc_near[here, :], 0.0)
        back_near[pl.ds(at_start, ch), :] += jnp.where(lane >= start_at, doc_back[here, :], 0.0)
        return carry

    lax.fori_loop(0, docs, add_docs, 0, unroll=4)

    wide = GROUP * ch

    def collect(c, order_row, source, by, delta, empty):
        tiles = []
        for i in range(GROUP):
            k = c * GROUP + i
            inside = table_ref[order_row + 2, k] >= delta
            at = jnp.where(inside, table_ref[order_row, k] + by, empty)
            tiles.append(source[pl.ds(pl.multiple_of(at * ch, ch), ch), :])
        return jnp.concatenate(tiles, axis=0)

    def outer(c, carry):
        here = pl.ds(pl.multiple_of(c * wide, wide), wide)
        reach_back, reach_ahead = table_ref[7, c * GROUP], table_ref[11, c * GROUP]

        @pl.when(reach_back == 0)
        def _():
            far_sum[here, :] = jnp.zeros((wide, BLK), F32)

        @pl.when(reach_ahead == 0)
        def _():
            back_far[here, :] = jnp.zeros((wide, BLK), F32)

        for reach in range(1, HOPS + 1):

            @pl.when(reach_back == reach)
            def _():
                x = jnp.concatenate(
                    [collect(c, 5, x_tail, HOPS - n, n, 0) for n in range(reach, 0, -1)], axis=1
                )
                lags = slice((HOPS - reach) * BLK, far)
                far_sum[here, :] = dot(x, fwd_ref[lags, :])
                pairs[:, lags] += dot(turned[:, here], x)

            @pl.when(reach_ahead == reach)
            def _():
                z = jnp.concatenate(
                    [collect(c, 9, z_head, n, n, blocks) for n in range(1, reach + 1)], axis=1
                )
                back_far[here, :] = dot(z, bwd_ref[BLK : (reach + 1) * BLK, :])

        return carry

    lax.fori_loop(0, blocks // GROUP, outer, 0)

    def gather_out(k, carry):
        b = table_ref[5, k]
        src, at_lane = place_of(b, peers)
        here = pl.ds(pl.multiple_of(k * ch, ch), ch)
        at = pl.multiple_of(b * ch, ch)
        ahead = jnp.where(lane < table_ref[1, b], far_sum[here, :], 0.0)
        ahead_at = pl.multiple_of(table_ref[10, b] * ch, ch)
        behind = jnp.where(lane >= table_ref[2, b], back_far[pl.ds(ahead_at, ch), :], 0.0)
        out_ref[src, 0, :, pl.ds(at_lane, BLK)] = (near[pl.ds(at, ch), :] + ahead).astype(BF16)
        out_ref[src, 1, :, pl.ds(at_lane, BLK)] = (back_near[pl.ds(at, ch), :] + behind).astype(BF16)
        return carry

    lax.fori_loop(0, blocks, gather_out, 0, unroll=4)

    total = jnp.zeros((8, far + 2 * BLK), F32)
    for r in range(BLK // 8):
        band = jnp.concatenate([pairs[8 * r : 8 * (r + 1), :], jnp.zeros((8, BLK), F32)], axis=1)
        total = total + pltpu.roll(band, BLK - 8 - 8 * r, 1)
    lags = total[7:8]
    for r in range(7):
        lags = lags + pltpu.roll(total[r : r + 1], 7 - r, 1)
    extra[...] = jnp.zeros_like(extra)
    count = TAP_ROWS
    for r in range(count):
        at = far + BLK - LANES * (r + 1)
        extra[r : r + 1, :] = lags[:, at : at + LANES]
    r_id = lax.broadcasted_iota(jnp.int32, (LANES, LANES), 0)
    c_id = lax.broadcasted_iota(jnp.int32, (LANES, LANES), 1)
    anti = jnp.where(r_id + c_id == LANES - 1, 1.0, 0.0).astype(BF16)
    extra[...] = dot(extra[...].astype(BF16), anti)

    by_channel = jnp.sum(skip, axis=1, keepdims=True)
    e_row = lax.broadcasted_iota(jnp.int32, (ch, LANES), 0)
    e_col = lax.broadcasted_iota(jnp.int32, (ch, LANES), 1)
    mine = e_row + ch * lax.rem(me_ref[0], LANES // ch) == e_col
    skip_row = jnp.sum(jnp.where(mine, by_channel, 0.0), axis=0, keepdims=True)
    high = skip_row.astype(BF16).astype(F32)
    extra[count : count + 1, :] = high
    extra[count + 1 : count + 2, :] = skip_row - high
    packed = extra[...].astype(BF16)
    for side in range(2):
        out_ref[:, side, :, 2 * BLK : 2 * BLK + LANES] = jnp.broadcast_to(
            packed[side * ch : (side + 1) * ch][None], (peers, ch, LANES)
        )


def finish_kernel(
    code_ref, slot_ref, gain_ref, own_ref, low_ref, high_ref, grad_ref,
    low_kv_ref, high_kv_ref, got_ref, y_ref, grads_ref,
    row, grad, got, y_row, grads_row, in_sems, out_sems,
):
    _, peers, _, chans, toks = got.shape

    def here(o):
        return pl.ds(o * toks, toks)

    def fetch(o, act):
        code = code_ref[o]

        @pl.when(code == 0)
        def _():
            act(pltpu.make_async_copy(own_ref.at[slot_ref[o]], row.at[o], in_sems.at[o, 0]))

        for n, first, later in ((1, low_ref, low_kv_ref), (2, high_ref, high_kv_ref)):

            @pl.when(code == n)
            def _():
                act(pltpu.make_async_copy(first.at[0], row.at[o, 0], in_sems.at[o, 0]))
                act(pltpu.make_async_copy(later, row.at[o, pl.ds(1, 2)], in_sems.at[o, 1]))

        act(pltpu.make_async_copy(grad_ref.at[here(o)], grad.at[o], in_sems.at[o, 2]))
        act(pltpu.make_async_copy(got_ref.at[:, :, :, here(o)], got.at[o], in_sems.at[o, 3]))

    def results(o, act):
        act(pltpu.make_async_copy(y_row.at[o], y_ref.at[here(o)], out_sems.at[o, 0]))
        for n in range(3):
            act(
                pltpu.make_async_copy(
                    grads_row.at[o, n], grads_ref.at[n, here(o)], out_sems.at[o, 1 + n]
                )
            )

    together = WIDE // chans
    for o in range(ROWS):
        fetch(o, lambda copy: copy.start())
    for o in range(ROWS):
        fetch(o, lambda copy: copy.wait())
        for n in range(peers // together):
            lanes = slice(n * WIDE, (n + 1) * WIDE)
            of = slice(n * together, (n + 1) * together)
            conv = got[o, of, 0].reshape(WIDE, toks).T.astype(F32)
            back = got[o, of, 1].reshape(WIDE, toks).T.astype(F32)
            query, key_in, value = (row[o, s, :, lanes].astype(F32) for s in range(3))
            out_grad = grad[o, :, lanes].astype(F32)
            gain = gain_ref[:, lanes]
            product = (key_in * value).astype(BF16).astype(F32)
            grad_mid = (out_grad * query).astype(BF16).astype(F32)
            mixed = conv + gain * product
            grad_x = back + gain * grad_mid
            y_row[o, :, lanes] = (query * mixed).astype(BF16)
            grads_row[o, 0, :, lanes] = (out_grad * mixed).astype(BF16)
            grads_row[o, 1, :, lanes] = (grad_x * value).astype(BF16)
            grads_row[o, 2, :, lanes] = (grad_x * key_in).astype(BF16)
        results(o, lambda copy: copy.start())
    for o in range(ROWS):
        results(o, lambda copy: copy.wait())


def totals_kernel(tap_scale, skip_scale, part_ref, taps_ref, skip_ref):
    filters = taps_ref.shape[0]
    peers, _, ch, lanes = part_ref.shape
    group = peers // filters
    for f in range(filters):
        part = part_ref[f * group : (f + 1) * group].astype(F32)
        total = jnp.sum(part, axis=0) * tap_scale
        for r in range(TAP_ROWS):
            row = total[r // ch, r % ch : r % ch + 1]
            taps_ref[f : f + 1, r * lanes : (r + 1) * lanes] = row
    at = TAP_ROWS - ch
    together = lanes // ch
    for r in range(peers // together):
        part = part_ref[r * together : (r + 1) * together, 1, :, :].astype(F32)
        total = jnp.sum(part, axis=0) * skip_scale
        skip_ref[r : r + 1, :] = total[at : at + 1] + total[at + 1 : at + 2]


def shifted(array, axis, by):
    length = lax.axis_size(axis)
    return lax.ppermute(array, axis, [(i, (i + by) % length) for i in range(length)])


def on_device(rollout_rows, pack_targets, doc_lengths, filter_taps, skip_gain, out_grad):
    peers = lax.axis_size("ctx")
    index = lax.axis_index("ctx").astype(jnp.int32)
    slots, row_len, streams, channels = rollout_rows.shape
    tokens = out_grad.shape[0]
    filters, tap_count = filter_taps.shape
    docs = doc_lengths.shape[0]
    ch = channels // peers
    blocks = 2 * peers
    own = rollout_rows.transpose(0, 2, 1, 3)
    half_shape = jax.ShapeDtypeStruct((2, row_len, channels), BF16)
    up, down, code, slot = pl.pallas_call(
        functools.partial(choose_kernel, peers),
        out_shape=(
            half_shape,
            half_shape,
            jax.ShapeDtypeStruct((ROWS,), jnp.int32),
            jax.ShapeDtypeStruct((ROWS + 2,), jnp.int32),
        ),
        in_specs=[smem(), smem(), hbm()],
        out_specs=(vmem(), vmem(), smem(), smem()),
        scratch_shapes=[
            VMEM((2, streams, row_len, channels), BF16),
            pltpu.SemaphoreType.DMA((2, 3)),
        ],
        compiler_params=pltpu.CompilerParams(vmem_limit_bytes=VLIM),
        name="choose",
    )(index[None], pack_targets.T, own)
    up_kv, down_kv = pl.pallas_call(
        later_kernel,
        out_shape=(half_shape, half_shape),
        in_specs=[smem(), hbm()],
        out_specs=(vmem(), vmem()),
        scratch_shapes=[pltpu.SemaphoreType.DMA((2,))],
        compiler_params=pltpu.CompilerParams(vmem_limit_bytes=VLIM),
        cost_estimate=pl.CostEstimate(flops=0, bytes_accessed=6_000_000, transcendentals=0),
        name="later",
    )(slot, own)
    low = shifted(up, "ctx", 1)
    high = shifted(down, "ctx", -1)

    mine = lax.dynamic_index_in_dim(filter_taps, index // (peers // filters), 0, keepdims=True)
    mine = mine.astype(BF16).astype(F32)
    mine = jnp.pad(mine, [(0, 0), (BLK, BLK * (HOPS + 1) - tap_count)])
    table = pl.pallas_call(
        functools.partial(tables_kernel, docs),
        out_shape=jax.ShapeDtypeStruct((16, docs), jnp.int32),
        in_specs=[smem()],
        out_specs=smem(),
        scratch_shapes=[SMEM((2, HOPS + 1), jnp.int32)],
        compiler_params=pltpu.CompilerParams(vmem_limit_bytes=4 * 1024 * 1024),
        cost_estimate=pl.CostEstimate(flops=0, bytes_accessed=20_000_000, transcendentals=0),
        name="tables",
    )(doc_lengths)

    sent_shape = jax.ShapeDtypeStruct((peers, 2, ch, tokens), BF16)
    row_buffers = [
        VMEM((ROWS, streams, row_len, channels), BF16),
        VMEM((ROWS, row_len, channels), BF16),
    ]
    part = pl.pallas_call(
        own_kernel,
        out_shape=sent_shape,
        in_specs=[smem(), smem(), hbm(), hbm()],
        out_specs=vmem(),
        scratch_shapes=row_buffers + [pltpu.SemaphoreType.DMA((2 * ROWS,))],
        compiler_params=pltpu.CompilerParams(vmem_limit_bytes=VLIM),
        cost_estimate=pl.CostEstimate(flops=0, bytes_accessed=20_000_000, transcendentals=0),
        name="own_products",
    )(code, slot, own, out_grad)
    sent = pl.pallas_call(
        guest_kernel,
        out_shape=sent_shape,
        in_specs=[smem(), hbm(), hbm(), hbm(), hbm()],
        out_specs=hbm(),
        scratch_shapes=[
            VMEM((2, 2, row_len, channels), BF16),
            VMEM((2, row_len, channels), BF16),
            VMEM((2, peers, 2, ch, row_len), BF16),
            pltpu.SemaphoreType.DMA((2, 2)),
            pltpu.SemaphoreType.DMA((2, channels // WIDE)),
        ],
        input_output_aliases={4: 0},
        compiler_params=pltpu.CompilerParams(vmem_limit_bytes=VLIM),
        name="guest_products",
    )(code, low, high, out_grad, part)
    got = lax.all_to_all(sent, "ctx", 0, 0, tiled=True)
    up_kv, down_kv, got = lax.optimization_barrier((up_kv, down_kv, got))
    low_kv = shifted(up_kv, "ctx", 1)
    high_kv = shifted(down_kv, "ctx", -1)

    rows = blocks * ch
    pad = HOPS * ch
    reply = pl.pallas_call(
        long_kernel,
        out_shape=jax.ShapeDtypeStruct((peers, 2, ch, tokens + LANES), BF16),
        in_specs=[smem(), smem(), vmem(), vmem()],
        out_specs=vmem(),
        scratch_shapes=[
            VMEM((BLK * (HOPS + 1), BLK), BF16),
            VMEM((BLK * (HOPS + 1), BLK), BF16),
            VMEM((rows, BLK), BF16),
            VMEM((rows, BLK), BF16),
            VMEM((rows + pad, BLK), BF16),
            VMEM((rows + pad, BLK), BF16),
            VMEM((rows, BLK), BF16),
            VMEM((rows, BLK), BF16),
            VMEM((rows, BLK), BF16),
            VMEM((rows, BLK), BF16),
            VMEM((BLK, rows), BF16),
            VMEM((rows, BLK), F32),
            VMEM((rows, BLK), F32),
            VMEM((rows, BLK), F32),
            VMEM((rows, BLK), F32),
            VMEM((rows, BLK), F32),
            VMEM((rows, BLK), F32),
            VMEM((BLK, BLK * (HOPS + 1)), F32),
            VMEM((2 * ch, LANES), F32),
        ],
        compiler_params=pltpu.CompilerParams(vmem_limit_bytes=34 * 1024 * 1024),
        cost_estimate=pl.CostEstimate(
            flops=2 * 30 * rows * BLK * BLK, bytes_accessed=7_000_000, transcendentals=0
        ),
        name="long_filter",
    )(index[None], table, got, mine)
    low_kv, high_kv, reply = lax.optimization_barrier((low_kv, high_kv, reply))
    back = lax.all_to_all(reply, "ctx", 0, 0, tiled=True)

    seq_total = tokens * peers
    chan_total = channels * lax.axis_size("ch")
    tap_sum, skip_sum = pl.pallas_call(
        functools.partial(
            totals_kernel,
            1.0 / math.sqrt(seq_total * chan_total / filters),
            1.0 / math.sqrt(seq_total),
        ),
        out_shape=(
            jax.ShapeDtypeStruct((filters, TAP_ROWS * LANES), F32),
            jax.ShapeDtypeStruct((channels // LANES, LANES), F32),
        ),
        grid=(1,),
        in_specs=[
            pl.BlockSpec((peers, 2, ch, LANES), lambda o: (0, 0, 0, tokens // LANES)),
        ],
        out_specs=(
            pl.BlockSpec((filters, TAP_ROWS * LANES), lambda o: (0, 0)),
            pl.BlockSpec((channels // LANES, LANES), lambda o: (0, 0)),
        ),
        name="totals",
    )(back)
    other = lax.ppermute(tap_sum, "ch", [(0, 1), (1, 0)])

    out_y, grads = pl.pallas_call(
        finish_kernel,
        out_shape=(
            jax.ShapeDtypeStruct((tokens, channels), BF16),
            jax.ShapeDtypeStruct((streams, tokens, channels), BF16),
        ),
        in_specs=[smem(), smem(), vmem()] + [hbm()] * 7,
        out_specs=(hbm(), hbm()),
        scratch_shapes=row_buffers
        + [
            VMEM((ROWS, peers, 2, ch, row_len), BF16),
            VMEM((ROWS, row_len, channels), BF16),
            VMEM((ROWS, streams, row_len, channels), BF16),
            pltpu.SemaphoreType.DMA((ROWS, 4)),
            pltpu.SemaphoreType.DMA((ROWS, 4)),
        ],
        compiler_params=pltpu.CompilerParams(vmem_limit_bytes=VLIM),
        name="finish",
    )(code, slot, skip_gain[None], own, low, high, out_grad, low_kv, high_kv, back)

    grad_taps = (tap_sum + other)[:, :tap_count]
    grad_skip = skip_sum.reshape(channels)
    return (out_y, grads.transpose(1, 0, 2), grad_taps, grad_skip)


def solution(mesh):
    return jax.shard_map(
        on_device,
        mesh=mesh,
        in_specs=(P("ctx", None, None, "ch"), P(), P(), P(), P("ch"), P("ctx", "ch")),
        out_specs=(P("ctx", "ch"), P("ctx", None, "ch"), P(), P("ch")),
        check_vma=False,
    )
```

```python
import functools
import math

import jax
import jax.numpy as jnp
from jax import lax
from jax.experimental import pallas as pl
from jax.experimental.pallas import tpu as pltpu
from jax.sharding import PartitionSpec as P

BF16 = jnp.bfloat16
F32 = jnp.float32
SMEM = pltpu.SMEM
VMEM = pltpu.VMEM

BLK = 256
HOPS = 8
SLOTS = 6
ROWS = 4
LANES = 128
WIDE = 128
GROUP = 32
TAP_ROWS = 17
VLIM = 56 * 1024 * 1024


def hbm():
    return pl.BlockSpec(memory_space=pltpu.HBM)


def smem():
    return pl.BlockSpec(memory_space=SMEM)


def vmem():
    return pl.BlockSpec(memory_space=VMEM)


def choose_kernel(
    cycle, me_ref, target_ref, own_ref, up_ref, down_ref, code_ref, slot_ref, rows, sems
):
    me = me_ref[0]
    below = lax.rem(me + cycle - 1, cycle)
    above = lax.rem(me + 1, cycle)
    up_slot = jnp.int32(0)
    down_slot = jnp.int32(0)
    for k in range(SLOTS):
        shard = target_ref[0, me * SLOTS + k]
        up_slot = jnp.where(shard == above, k, up_slot)
        down_slot = jnp.where(shard == below, k, down_slot)
    copies = [
        pltpu.make_async_copy(own_ref.at[slot, n], rows.at[side, n], sems.at[side, n])
        for side, slot in enumerate((up_slot, down_slot))
        for n in range(3)
    ]
    for copy in copies:
        copy.start()
    for o in range(ROWS):
        code_ref[o] = 0
        slot_ref[o] = 0
    slot_ref[ROWS] = up_slot
    slot_ref[ROWS + 1] = down_slot
    for k in range(SLOTS):
        shard = target_ref[0, me * SLOTS + k]
        offset = target_ref[1, me * SLOTS + k]

        @pl.when(shard == me)
        def _():
            slot_ref[offset] = k

        for owner, code in ((below, 1), (above, 2)):
            their_shard = target_ref[0, owner * SLOTS + k]
            their_offset = target_ref[1, owner * SLOTS + k]

            @pl.when(their_shard == me)
            def _():
                code_ref[their_offset] = code

    for copy in copies:
        copy.wait()
    for side, to_ref in enumerate((up_ref, down_ref)):
        to_ref[0] = rows[side, 0]
        for n in range(rows.shape[-1] // WIDE):
            lanes = slice(n * WIDE, (n + 1) * WIDE)
            to_ref[1, :, lanes] = round_mul(rows[side, 1, :, lanes], rows[side, 2, :, lanes])


def later_kernel(slot_ref, own_ref, up_ref, down_ref, sems):
    copies = [
        pltpu.make_async_copy(own_ref.at[slot_ref[ROWS + n], pl.ds(1, 2)], to_ref, sems.at[n])
        for n, to_ref in enumerate((up_ref, down_ref))
    ]
    for copy in copies:
        copy.start()
    for copy in copies:
        copy.wait()


def tables_kernel(docs, length_ref, table_ref, count_ref):
    def one_doc(d, start):
        end = start + length_ref[d]
        table_ref[3, d] = start
        table_ref[4, d] = end

        def heads(b, carry):
            table_ref[0, b] = b - lax.shift_right_logical(start, 8)
            table_ref[1, b] = jnp.minimum(end - BLK * b, BLK)
            return carry

        def tails(b, carry):
            table_ref[2, b] = jnp.maximum(start - BLK * b, 0)
            table_ref[8, b] = lax.shift_right_logical(end - 1, 8) - b
            return carry

        lax.fori_loop(
            lax.shift_right_logical(start + BLK - 1, 8),
            lax.shift_right_logical(end + BLK - 1, 8),
            heads,
            0,
        )
        lax.fori_loop(
            lax.shift_right_logical(start, 8), lax.shift_right_logical(end, 8), tails, 0
        )
        return end

    lax.fori_loop(0, docs, one_doc, jnp.int32(0))

    for kind, (reach_row, order_row) in enumerate(((0, 5), (8, 9))):
        for n in range(HOPS + 1):
            count_ref[kind, n] = 0

        def count(b, carry):
            reach = table_ref[reach_row, b]
            count_ref[kind, reach] = count_ref[kind, reach] + 1
            return carry

        lax.fori_loop(0, docs, count, 0)
        before = jnp.int32(0)
        for n in range(HOPS, -1, -1):
            these = count_ref[kind, n]
            count_ref[kind, n] = before
            before = before + these

        def place(b, carry):
            reach = table_ref[reach_row, b]
            at = count_ref[kind, reach]
            count_ref[kind, reach] = at + 1
            table_ref[order_row, at] = b
            table_ref[order_row + 1, b] = at
            table_ref[order_row + 2, at] = reach
            return carry

        lax.fori_loop(0, docs, place, 0)


def make_bands(taps_ref, fwd_ref, bwd_ref):
    width = BLK * (HOPS + 2)
    part = 32
    for r in range(BLK // part):
        rows = jnp.broadcast_to(taps_ref[...], (part, width))
        rows = pltpu.roll(rows, part * r, 1, stride=1, stride_axis=0)
        for delta in range(HOPS + 1):
            at = BLK * (HOPS - delta) + part * r
            fwd_ref[at : at + part, :] = rows[:, BLK * (delta + 1) : BLK * (delta + 2)].astype(BF16)
    for delta in range(HOPS + 1):
        at = BLK * (HOPS - delta)
        bwd_ref[BLK * delta : BLK * (delta + 1), :] = fwd_ref[at : at + BLK, :].T


def round_mul(a, b):
    return (a.astype(F32) * b.astype(F32)).astype(BF16)


def write_row(sent_ref, lane, toks, read_product, read_grad_mid):
    peers, _, chans, _ = sent_ref.shape
    together = WIDE // chans
    for n in range(peers // together):
        lanes = slice(n * WIDE, (n + 1) * WIDE)
        to = slice(n * together, (n + 1) * together)
        for side, read in enumerate((read_product, read_grad_mid)):
            sent_ref[to, side, :, lane : lane + toks] = read(lanes).T.reshape(together, chans, toks)


def own_kernel(code_ref, slot_ref, own_ref, grad_ref, sent_ref, row, grad, sems):
    toks = row.shape[2]

    def copies(o):
        return (
            pltpu.make_async_copy(own_ref.at[slot_ref[o]], row.at[o], sems.at[o]),
            pltpu.make_async_copy(
                grad_ref.at[pl.ds(o * toks, toks)], grad.at[o], sems.at[ROWS + o]
            ),
        )

    for o in range(ROWS):
        for copy in copies(o):
            copy.start()
    for o in range(ROWS):
        for copy in copies(o):
            copy.wait()

        @pl.when(code_ref[o] == 0)
        def _():
            write_row(
                sent_ref,
                o * toks,
                toks,
                lambda c: round_mul(row[o, 1, :, c], row[o, 2, :, c]),
                lambda c: round_mul(grad[o, :, c], row[o, 0, :, c]),
            )


def guest_kernel(
    code_ref, low_ref, high_ref, grad_ref, part_ref, sent_ref, guest, grad, ready, in_sems, out_sems
):
    del part_ref
    _, peers, _, chans, toks = ready.shape
    together = WIDE // chans
    parts = peers // together
    guests = []
    for n, ref in enumerate((low_ref, high_ref)):
        at = jnp.int32(0)
        for o in range(ROWS):
            at = jnp.where(code_ref[o] == n + 1, o + 1, at)
        here = pl.ds(pl.multiple_of(jnp.maximum(at - 1, 0) * toks, toks), toks)
        into = [
            pltpu.make_async_copy(ref, guest.at[n], in_sems.at[n, 0]),
            pltpu.make_async_copy(grad_ref.at[here], grad.at[n], in_sems.at[n, 1]),
        ]
        out = []
        for m in range(parts):
            to = pl.ds(m * together, together)
            out.append(
                pltpu.make_async_copy(
                    ready.at[n, to], sent_ref.at[to, :, :, here], out_sems.at[n, m]
                )
            )
        guests.append((n, at > 0, into, out))
    for n, live, into, out in guests:

        @pl.when(live)
        def _():
            for copy in into:
                copy.start()

    for n, live, into, out in guests:

        @pl.when(live)
        def _():
            for copy in into:
                copy.wait()
            for m in range(parts):
                lanes = slice(m * WIDE, (m + 1) * WIDE)
                to = slice(m * together, (m + 1) * together)
                grad_mid = round_mul(grad[n, :, lanes], guest[n, 0, :, lanes])
                ready[n, to, 0] = guest[n, 1, :, lanes].T.reshape(together, chans, toks)
                ready[n, to, 1] = grad_mid.T.reshape(together, chans, toks)
                out[m].start()

    for n, live, into, out in guests:

        @pl.when(live)
        def _():
            for copy in out:
                copy.wait()


def place_of(b, peers):
    src = jnp.where(b < peers, b, 2 * peers - 1 - b)
    lane = pl.multiple_of(jnp.where(b < peers, 0, BLK), BLK)
    return src, lane


def dot(a, b):
    return jnp.dot(a, b, preferred_element_type=F32)


def long_kernel(
    me_ref, table_ref, got_ref, taps_ref, out_ref,
    fwd_ref, bwd_ref, x_all, z_all, x_tail, z_head, z_back, xd, zd, ze, turned, doc_near, doc_back,
    near, far_sum, back_near, back_far, pairs, extra,
):
    peers = got_ref.shape[0]
    ch = got_ref.shape[2]
    blocks = 2 * peers
    docs = blocks
    rows = blocks * ch
    pad = HOPS * ch
    far = HOPS * BLK
    lane = lax.broadcasted_iota(jnp.int32, (ch, BLK), 1)

    make_bands(taps_ref, fwd_ref, bwd_ref)
    x_tail[0:pad, :] = jnp.zeros((pad, BLK), BF16)
    z_head[rows : rows + pad, :] = jnp.zeros((pad, BLK), BF16)
    pairs[...] = jnp.zeros_like(pairs)

    def spread(k, total):
        b = table_ref[5, k]
        src, at_lane = place_of(b, peers)
        at = pl.multiple_of(b * ch, ch)
        x = got_ref[src, 0, :, pl.ds(at_lane, BLK)]
        z = got_ref[src, 1, :, pl.ds(at_lane, BLK)]
        x_all[pl.ds(at, ch), :] = x
        z_all[pl.ds(at, ch), :] = z
        end, tail = table_ref[1, b], table_ref[2, b]
        x_f, z_f = x.astype(F32), z.astype(F32)
        x_tail[pl.ds(at + pad, ch), :] = jnp.where(lane >= tail, x_f, 0).astype(BF16)
        z_cut = jnp.where(lane < end, z_f, 0).astype(BF16)
        z_head[pl.ds(at, ch), :] = z_cut
        z_back[pl.ds(pl.multiple_of(k * ch, ch), ch), :] = z_cut
        return total + x_f * z_f

    skip = lax.fori_loop(0, blocks, spread, jnp.zeros((ch, BLK), F32), unroll=4)

    def doc_parts(d):
        start, end = table_ref[3, d], table_ref[4, d]
        end_block = lax.shift_right_logical(end - 1, 8)
        end_at = jnp.bitwise_and(end, BLK - 1)
        end_from = jnp.maximum(start - BLK * end_block, 0)
        start_block = lax.shift_right_logical(start, 8)
        start_at = jnp.bitwise_and(start, BLK - 1)
        start_at = jnp.where(start_at == 0, BLK, start_at)
        start_to = end - BLK * start_block
        return end_block, end_from, end_at, start_block, start_at, start_to

    def spread_docs(d, carry):
        end_block, end_from, end_at, start_block, start_at, start_to = doc_parts(d)
        at = pl.multiple_of(d * ch, ch)
        at_end = pl.multiple_of(end_block * ch, ch)
        at_start = pl.multiple_of(start_block * ch, ch)
        ends = (lane >= end_from) & (lane < end_at)
        begins = (lane >= start_at) & (lane < start_to)
        x = x_all[pl.ds(at_end, ch), :].astype(F32)
        z = z_all[pl.ds(at_end, ch), :].astype(F32)
        z2 = z_all[pl.ds(at_start, ch), :].astype(F32)
        xd[pl.ds(at, ch), :] = jnp.where(ends, x, 0).astype(BF16)
        zd[pl.ds(at, ch), :] = jnp.where(ends, z, 0).astype(BF16)
        ze[pl.ds(at, ch), :] = jnp.where(begins, z2, 0).astype(BF16)
        return carry

    lax.fori_loop(0, docs, spread_docs, 0, unroll=4)

    step = 512
    first_fwd = fwd_ref.at[far : far + BLK, :]
    first_bwd = bwd_ref.at[0:BLK, :]

    def inner(c, carry):
        at = pl.multiple_of(c * step, step)
        here = pl.ds(at, step)
        z = z_head[here, :]
        x = jnp.concatenate([x_tail[pl.ds(at + pad, step), :], xd[here, :]], axis=0)
        ahead = dot(x, first_fwd[...])
        near[here, :] = ahead[:step]
        doc_near[here, :] = ahead[step:]
        behind = dot(jnp.concatenate([z, ze[here, :]], axis=0), first_bwd[...])
        back_near[here, :] = behind[:step]
        doc_back[here, :] = behind[step:]
        turned[:, here] = z_back[here, :].T
        pairs[:, far:] += dot(jnp.concatenate([z_all[here, :].T, zd[here, :].T], axis=1), x)
        return carry

    lax.fori_loop(0, rows // step, inner, 0)

    def add_docs(d, carry):
        end_block, end_from, end_at, start_block, start_at, start_to = doc_parts(d)
        here = pl.ds(pl.multiple_of(d * ch, ch), ch)
        at_end = pl.multiple_of(end_block * ch, ch)
        at_start = pl.multiple_of(start_block * ch, ch)
        near[pl.ds(at_end, ch), :] += jnp.where(lane < end_at, doc_near[here, :], 0.0)
        back_near[pl.ds(at_start, ch), :] += jnp.where(lane >= start_at, doc_back[here, :], 0.0)
        return carry

    lax.fori_loop(0, docs, add_docs, 0, unroll=4)

    wide = GROUP * ch

    def collect(c, order_row, source, by, delta, empty):
        tiles = []
        for i in range(GROUP):
            k = c * GROUP + i
            inside = table_ref[order_row + 2, k] >= delta
            at = jnp.where(inside, table_ref[order_row, k] + by, empty)
            tiles.append(source[pl.ds(pl.multiple_of(at * ch, ch), ch), :])
        return jnp.concatenate(tiles, axis=0)

    def outer(c, carry):
        here = pl.ds(pl.multiple_of(c * wide, wide), wide)
        reach_back, reach_ahead = table_ref[7, c * GROUP], table_ref[11, c * GROUP]

        @pl.when(reach_back == 0)
        def _():
            far_sum[here, :] = jnp.zeros((wide, BLK), F32)

        @pl.when(reach_ahead == 0)
        def _():
            back_far[here, :] = jnp.zeros((wide, BLK), F32)

        for reach in range(1, HOPS + 1):

            @pl.when(reach_back == reach)
            def _():
                x = jnp.concatenate(
                    [collect(c, 5, x_tail, HOPS - n, n, 0) for n in range(reach, 0, -1)], axis=1
                )
                lags = slice((HOPS - reach) * BLK, far)
                far_sum[here, :] = dot(x, fwd_ref[lags, :])
                pairs[:, lags] += dot(turned[:, here], x)

            @pl.when(reach_ahead == reach)
            def _():
                z = jnp.concatenate(
                    [collect(c, 9, z_head, n, n, blocks) for n in range(1, reach + 1)], axis=1
                )
                back_far[here, :] = dot(z, bwd_ref[BLK : (reach + 1) * BLK, :])

        return carry

    lax.fori_loop(0, blocks // GROUP, outer, 0)

    def gather_out(k, carry):
        b = table_ref[5, k]
        src, at_lane = place_of(b, peers)
        here = pl.ds(pl.multiple_of(k * ch, ch), ch)
        at = pl.multiple_of(b * ch, ch)
        ahead = jnp.where(lane < table_ref[1, b], far_sum[here, :], 0.0)
        ahead_at = pl.multiple_of(table_ref[10, b] * ch, ch)
        behind = jnp.where(lane >= table_ref[2, b], back_far[pl.ds(ahead_at, ch), :], 0.0)
        out_ref[src, 0, :, pl.ds(at_lane, BLK)] = (near[pl.ds(at, ch), :] + ahead).astype(BF16)
        out_ref[src, 1, :, pl.ds(at_lane, BLK)] = (back_near[pl.ds(at, ch), :] + behind).astype(BF16)
        return carry

    lax.fori_loop(0, blocks, gather_out, 0, unroll=4)

    total = jnp.zeros((8, far + 2 * BLK), F32)
    for r in range(BLK // 8):
        band = jnp.concatenate([pairs[8 * r : 8 * (r + 1), :], jnp.zeros((8, BLK), F32)], axis=1)
        total = total + pltpu.roll(band, BLK - 8 - 8 * r, 1)
    lags = total[7:8]
    for r in range(7):
        lags = lags + pltpu.roll(total[r : r + 1], 7 - r, 1)
    extra[...] = jnp.zeros_like(extra)
    count = TAP_ROWS
    for r in range(count):
        at = far + BLK - LANES * (r + 1)
        extra[r : r + 1, :] = lags[:, at : at + LANES]
    r_id = lax.broadcasted_iota(jnp.int32, (LANES, LANES), 0)
    c_id = lax.broadcasted_iota(jnp.int32, (LANES, LANES), 1)
    anti = jnp.where(r_id + c_id == LANES - 1, 1.0, 0.0).astype(BF16)
    extra[...] = dot(extra[...].astype(BF16), anti)

    by_channel = jnp.sum(skip, axis=1, keepdims=True)
    e_row = lax.broadcasted_iota(jnp.int32, (ch, LANES), 0)
    e_col = lax.broadcasted_iota(jnp.int32, (ch, LANES), 1)
    mine = e_row + ch * lax.rem(me_ref[0], LANES // ch) == e_col
    skip_row = jnp.sum(jnp.where(mine, by_channel, 0.0), axis=0, keepdims=True)
    high = skip_row.astype(BF16).astype(F32)
    extra[count : count + 1, :] = high
    extra[count + 1 : count + 2, :] = skip_row - high
    packed = extra[...].astype(BF16)
    for side in range(2):
        out_ref[:, side, :, 2 * BLK : 2 * BLK + LANES] = jnp.broadcast_to(
            packed[side * ch : (side + 1) * ch][None], (peers, ch, LANES)
        )


def finish_kernel(
    code_ref, slot_ref, gain_ref, own_ref, low_ref, high_ref, grad_ref,
    low_kv_ref, high_kv_ref, got_ref, y_ref, grads_ref,
    row, grad, got, y_row, grads_row, in_sems, out_sems,
):
    _, peers, _, chans, toks = got.shape

    def here(o):
        return pl.ds(o * toks, toks)

    def fetch(o, act):
        code = code_ref[o]

        @pl.when(code == 0)
        def _():
            act(pltpu.make_async_copy(own_ref.at[slot_ref[o]], row.at[o], in_sems.at[o, 0]))

        for n, first, later in ((1, low_ref, low_kv_ref), (2, high_ref, high_kv_ref)):

            @pl.when(code == n)
            def _():
                act(pltpu.make_async_copy(first.at[0], row.at[o, 0], in_sems.at[o, 0]))
                act(pltpu.make_async_copy(later, row.at[o, pl.ds(1, 2)], in_sems.at[o, 1]))

        act(pltpu.make_async_copy(grad_ref.at[here(o)], grad.at[o], in_sems.at[o, 2]))
        act(pltpu.make_async_copy(got_ref.at[:, :, :, here(o)], got.at[o], in_sems.at[o, 3]))

    def results(o, act):
        act(pltpu.make_async_copy(y_row.at[o], y_ref.at[here(o)], out_sems.at[o, 0]))
        for n in range(3):
            act(
                pltpu.make_async_copy(
                    grads_row.at[o, n], grads_ref.at[n, here(o)], out_sems.at[o, 1 + n]
                )
            )

    together = WIDE // chans
    for o in range(ROWS):
        fetch(o, lambda copy: copy.start())
    for o in range(ROWS):
        fetch(o, lambda copy: copy.wait())
        for n in range(peers // together):
            lanes = slice(n * WIDE, (n + 1) * WIDE)
            of = slice(n * together, (n + 1) * together)
            conv = got[o, of, 0].reshape(WIDE, toks).T.astype(F32)
            back = got[o, of, 1].reshape(WIDE, toks).T.astype(F32)
            query, key_in, value = (row[o, s, :, lanes].astype(F32) for s in range(3))
            out_grad = grad[o, :, lanes].astype(F32)
            gain = gain_ref[:, lanes]
            product = (key_in * value).astype(BF16).astype(F32)
            grad_mid = (out_grad * query).astype(BF16).astype(F32)
            mixed = conv + gain * product
            grad_x = back + gain * grad_mid
            y_row[o, :, lanes] = (query * mixed).astype(BF16)
            grads_row[o, 0, :, lanes] = (out_grad * mixed).astype(BF16)
            grads_row[o, 1, :, lanes] = (grad_x * value).astype(BF16)
            grads_row[o, 2, :, lanes] = (grad_x * key_in).astype(BF16)
        results(o, lambda copy: copy.start())
    for o in range(ROWS):
        results(o, lambda copy: copy.wait())


def totals_kernel(tap_scale, skip_scale, part_ref, taps_ref, skip_ref):
    filters = taps_ref.shape[0]
    peers, _, ch, lanes = part_ref.shape
    group = peers // filters
    for f in range(filters):
        part = part_ref[f * group : (f + 1) * group].astype(F32)
        total = jnp.sum(part, axis=0) * tap_scale
        for r in range(TAP_ROWS):
            row = total[r // ch, r % ch : r % ch + 1]
            taps_ref[f : f + 1, r * lanes : (r + 1) * lanes] = row
    at = TAP_ROWS - ch
    together = lanes // ch
    for r in range(peers // together):
        part = part_ref[r * together : (r + 1) * together, 1, :, :].astype(F32)
        total = jnp.sum(part, axis=0) * skip_scale
        skip_ref[r : r + 1, :] = total[at : at + 1] + total[at + 1 : at + 2]


def shifted(array, axis, by):
    length = lax.axis_size(axis)
    return lax.ppermute(array, axis, [(i, (i + by) % length) for i in range(length)])


def on_device(rollout_rows, pack_targets, doc_lengths, filter_taps, skip_gain, out_grad):
    peers = lax.axis_size("ctx")
    index = lax.axis_index("ctx").astype(jnp.int32)
    slots, row_len, streams, channels = rollout_rows.shape
    tokens = out_grad.shape[0]
    filters, tap_count = filter_taps.shape
    docs = doc_lengths.shape[0]
    ch = channels // peers
    blocks = 2 * peers
    own = rollout_rows.transpose(0, 2, 1, 3)
    half_shape = jax.ShapeDtypeStruct((2, row_len, channels), BF16)
    up, down, code, slot = pl.pallas_call(
        functools.partial(choose_kernel, peers),
        out_shape=(
            half_shape,
            half_shape,
            jax.ShapeDtypeStruct((ROWS,), jnp.int32),
            jax.ShapeDtypeStruct((ROWS + 2,), jnp.int32),
        ),
        in_specs=[smem(), smem(), hbm()],
        out_specs=(vmem(), vmem(), smem(), smem()),
        scratch_shapes=[
            VMEM((2, streams, row_len, channels), BF16),
            pltpu.SemaphoreType.DMA((2, 3)),
        ],
        compiler_params=pltpu.CompilerParams(vmem_limit_bytes=VLIM),
        name="choose",
    )(index[None], pack_targets.T, own)
    up_kv, down_kv = pl.pallas_call(
        later_kernel,
        out_shape=(half_shape, half_shape),
        in_specs=[smem(), hbm()],
        out_specs=(vmem(), vmem()),
        scratch_shapes=[pltpu.SemaphoreType.DMA((2,))],
        compiler_params=pltpu.CompilerParams(vmem_limit_bytes=VLIM),
        cost_estimate=pl.CostEstimate(flops=0, bytes_accessed=6_000_000, transcendentals=0),
        name="later",
    )(slot, own)
    low = shifted(up, "ctx", 1)
    high = shifted(down, "ctx", -1)

    mine = lax.dynamic_index_in_dim(filter_taps, index // (peers // filters), 0, keepdims=True)
    mine = mine.astype(BF16).astype(F32)
    mine = jnp.pad(mine, [(0, 0), (BLK, BLK * (HOPS + 1) - tap_count)])
    table = pl.pallas_call(
        functools.partial(tables_kernel, docs),
        out_shape=jax.ShapeDtypeStruct((16, docs), jnp.int32),
        in_specs=[smem()],
        out_specs=smem(),
        scratch_shapes=[SMEM((2, HOPS + 1), jnp.int32)],
        compiler_params=pltpu.CompilerParams(vmem_limit_bytes=4 * 1024 * 1024),
        cost_estimate=pl.CostEstimate(flops=0, bytes_accessed=20_000_000, transcendentals=0),
        name="tables",
    )(doc_lengths)

    sent_shape = jax.ShapeDtypeStruct((peers, 2, ch, tokens), BF16)
    row_buffers = [
        VMEM((ROWS, streams, row_len, channels), BF16),
        VMEM((ROWS, row_len, channels), BF16),
    ]
    part = pl.pallas_call(
        own_kernel,
        out_shape=sent_shape,
        in_specs=[smem(), smem(), hbm(), hbm()],
        out_specs=vmem(),
        scratch_shapes=row_buffers + [pltpu.SemaphoreType.DMA((2 * ROWS,))],
        compiler_params=pltpu.CompilerParams(vmem_limit_bytes=VLIM),
        cost_estimate=pl.CostEstimate(flops=0, bytes_accessed=20_000_000, transcendentals=0),
        name="own_products",
    )(code, slot, own, out_grad)
    sent = pl.pallas_call(
        guest_kernel,
        out_shape=sent_shape,
        in_specs=[smem(), hbm(), hbm(), hbm(), hbm()],
        out_specs=hbm(),
        scratch_shapes=[
            VMEM((2, 2, row_len, channels), BF16),
            VMEM((2, row_len, channels), BF16),
            VMEM((2, peers, 2, ch, row_len), BF16),
            pltpu.SemaphoreType.DMA((2, 2)),
            pltpu.SemaphoreType.DMA((2, channels // WIDE)),
        ],
        input_output_aliases={4: 0},
        compiler_params=pltpu.CompilerParams(vmem_limit_bytes=VLIM),
        name="guest_products",
    )(code, low, high, out_grad, part)
    got = lax.all_to_all(sent, "ctx", 0, 0, tiled=True)
    up_kv, down_kv, got = lax.optimization_barrier((up_kv, down_kv, got))
    low_kv = shifted(up_kv, "ctx", 1)
    high_kv = shifted(down_kv, "ctx", -1)

    rows = blocks * ch
    pad = HOPS * ch
    reply = pl.pallas_call(
        long_kernel,
        out_shape=jax.ShapeDtypeStruct((peers, 2, ch, tokens + LANES), BF16),
        in_specs=[smem(), smem(), vmem(), vmem()],
        out_specs=vmem(),
        scratch_shapes=[
            VMEM((BLK * (HOPS + 1), BLK), BF16),
            VMEM((BLK * (HOPS + 1), BLK), BF16),
            VMEM((rows, BLK), BF16),
            VMEM((rows, BLK), BF16),
            VMEM((rows + pad, BLK), BF16),
            VMEM((rows + pad, BLK), BF16),
            VMEM((rows, BLK), BF16),
            VMEM((rows, BLK), BF16),
            VMEM((rows, BLK), BF16),
            VMEM((rows, BLK), BF16),
            VMEM((BLK, rows), BF16),
            VMEM((rows, BLK), F32),
            VMEM((rows, BLK), F32),
            VMEM((rows, BLK), F32),
            VMEM((rows, BLK), F32),
            VMEM((rows, BLK), F32),
            VMEM((rows, BLK), F32),
            VMEM((BLK, BLK * (HOPS + 1)), F32),
            VMEM((2 * ch, LANES), F32),
        ],
        compiler_params=pltpu.CompilerParams(vmem_limit_bytes=34 * 1024 * 1024),
        cost_estimate=pl.CostEstimate(
            flops=2 * 30 * rows * BLK * BLK, bytes_accessed=7_000_000, transcendentals=0
        ),
        name="long_filter",
    )(index[None], table, got, mine)
    low_kv, high_kv, reply = lax.optimization_barrier((low_kv, high_kv, reply))
    back = lax.all_to_all(reply, "ctx", 0, 0, tiled=True)

    seq_total = tokens * peers
    chan_total = channels * lax.axis_size("ch")
    tap_sum, skip_sum = pl.pallas_call(
        functools.partial(
            totals_kernel,
            1.0 / math.sqrt(seq_total * chan_total / filters),
            1.0 / math.sqrt(seq_total),
        ),
        out_shape=(
            jax.ShapeDtypeStruct((filters, TAP_ROWS * LANES), F32),
            jax.ShapeDtypeStruct((channels // LANES, LANES), F32),
        ),
        grid=(1,),
        in_specs=[
            pl.BlockSpec((peers, 2, ch, LANES), lambda o: (0, 0, 0, tokens // LANES)),
        ],
        out_specs=(
            pl.BlockSpec((filters, TAP_ROWS * LANES), lambda o: (0, 0)),
            pl.BlockSpec((channels // LANES, LANES), lambda o: (0, 0)),
        ),
        name="totals",
    )(back)
    other = lax.ppermute(tap_sum, "ch", [(0, 1), (1, 0)])

    out_y, grads = pl.pallas_call(
        finish_kernel,
        out_shape=(
            jax.ShapeDtypeStruct((tokens, channels), BF16),
            jax.ShapeDtypeStruct((streams, tokens, channels), BF16),
        ),
        in_specs=[smem(), smem(), vmem()] + [hbm()] * 7,
        out_specs=(hbm(), hbm()),
        scratch_shapes=row_buffers
        + [
            VMEM((ROWS, peers, 2, ch, row_len), BF16),
            VMEM((ROWS, row_len, channels), BF16),
            VMEM((ROWS, streams, row_len, channels), BF16),
            pltpu.SemaphoreType.DMA((ROWS, 4)),
            pltpu.SemaphoreType.DMA((ROWS, 4)),
        ],
        compiler_params=pltpu.CompilerParams(vmem_limit_bytes=VLIM),
        name="finish",
    )(code, slot, skip_gain[None], own, low, high, out_grad, low_kv, high_kv, back)

    grad_taps = (tap_sum + other)[:, :tap_count]
    grad_skip = skip_sum.reshape(channels)
    return (out_y, grads.transpose(1, 0, 2), grad_taps, grad_skip)


def solution(mesh):
    return jax.shard_map(
        on_device,
        mesh=mesh,
        in_specs=(P("ctx", None, None, "ch"), P(), P(), P(), P("ch"), P("ctx", "ch")),
        out_specs=(P("ctx", "ch"), P("ctx", None, "ch"), P(), P("ch")),
        check_vma=False,
    )
```
